512 devices in a mesh: seq: 64 (over y, z), tp: 8 (over x, core).
Axes of the slice: x: 4, y: 4, z: 16, core: 2. Of those that a mesh axis runs over, the one named last changes fastest.
Arguments:
- queries: bfloat16 [32768, 2048], P('seq', 'tp'), may hold values from -5 to 5
- key_vectors: bfloat16 [32768, 2048], P('seq', 'tp'), may hold values from -5 to 5
- value_vectors: bfloat16 [32768, 2048], P('seq', 'tp'), may hold values from -5 to 5
- out_weight: bfloat16 [2048, 2048], P('tp'), may hold values from -0.125 to 0.125
- attn_grad: bfloat16 [32768, 2048], P('seq', 'tp'), may hold values from -5 to 5
- tile_column_mask: int32 [4, 64, 64], replicated, may hold values from 0 to 1, as said below
Outputs:
- projected: bfloat16 [32768, 2048], P('seq', 'tp')
- grad_queries: bfloat16 [32768, 2048], P('seq', 'tp')
- grad_keys: bfloat16 [32768, 2048], P('seq', 'tp')
- grad_values: bfloat16 [32768, 2048], P('seq', 'tp')
The draws below stay inside these ranges and needn't reach their ends.
Inputs may be any that keep to these rules, and one draw needn't show every extreme that they name: tile_column_mask[b, r, r'] is 0 where r' >= r and 1 where r - 2 <= r' < r.
All inputs are finite; a program needn't handle non-finite values.
Results may differ from the reference program's by a relative error of at most 0.02.
Values may be sent and summed in bfloat16 or wider, within the bound.
No kernel may reach another device: no remote copies, remote signals or barrier semaphores. Data moves between devices by JAX's collectives and lax.ppermute only.
A program may use at most 64 MiB of HBM per device.

```python
import jax
import jax.numpy as jnp
from jax import lax

D = 2048
HEAD_DIM = 128
COLS = 512
TILE = 128
ROWS = 64
TOKENS = 32768
N_TP = 8


def draw_queries(key, part):
    key = jax.random.fold_in(key, 11)
    return jax.random.truncated_normal(key, -4.5, 4.5, (TOKENS, D), jnp.float32).astype(jnp.bfloat16)


def draw_key_vectors(key, part):
    key = jax.random.fold_in(key, 23)
    return jax.random.truncated_normal(key, -4.5, 4.5, (TOKENS, D), jnp.float32).astype(jnp.bfloat16)


def draw_tile_column_mask(key, part):
    key = jax.random.fold_in(key, 37)
    density_key, entry_key = jax.random.split(key)
    block_count = COLS // TILE
    density = jax.random.randint(density_key, (block_count, 1, 1), 5, 96)
    entries = jax.random.randint(entry_key, (block_count, ROWS, ROWS), 0, 100)
    query_row = lax.broadcasted_iota(jnp.int32, (block_count, ROWS, ROWS), 1)
    key_row = lax.broadcasted_iota(jnp.int32, (block_count, ROWS, ROWS), 2)
    earlier = key_row < query_row
    nearest = earlier & (key_row >= query_row - 2)
    return jnp.where(nearest, 1, jnp.where(earlier & (entries < density), 1, 0)).astype(jnp.int32)


def shard_levels(own_key, extent, cuts, smallest, largest):
    factor_of = 1.0
    for dim, parts in cuts:
        heights = jax.random.uniform(jax.random.fold_in(jax.random.fold_in(own_key, 6), dim), (parts,), jnp.float32, smallest / len(cuts), largest / len(cuts))
        factor_of = factor_of * jnp.repeat(jnp.exp(heights), extent[dim] // parts).reshape((-1,) + (1,) * (len(extent) - 1 - dim))
    return factor_of


def normal_values(rng, extent, scale, most, cuts=(), kind=jnp.bfloat16):
    values = scale * jax.random.normal(rng, extent, jnp.float32)
    if cuts:
        values = values * shard_levels(rng, extent, cuts, -0.22, 0.18)
    return jnp.clip(values, -most, most).astype(kind)


def setup_inputs(seed: int = 0) -> dict:
    arg_keys = jax.random.split(jax.random.key(seed), 7)
    return {
        "queries": draw_queries(jax.random.fold_in(arg_keys[6], 71), 0),
        "key_vectors": draw_key_vectors(jax.random.fold_in(arg_keys[6], 71), 0),
        "value_vectors": normal_values(arg_keys[2], (TOKENS, D), 1.0, 5.0, ((0, 64), (1, 8))),
        "out_weight": normal_values(arg_keys[3], (D, D), D ** -0.5, 0.125, ((0, 8),)),
        "attn_grad": normal_values(arg_keys[4], (TOKENS, D), 1.0, 5.0, ((0, 64), (1, 8))),
        "tile_column_mask": draw_tile_column_mask(jax.random.fold_in(arg_keys[6], 71), 0),
    }


negative_fill = -1e30


def rounded(values_in):
    return lax.optimization_barrier(values_in.astype(jnp.bfloat16)).astype(jnp.float32)


def partial_attention(scores, allowed, value_block, out_form):
    masked = jnp.where(allowed, scores, negative_fill)
    maxima = jnp.max(masked, axis=-1)
    weights = jnp.where(allowed, jnp.exp(masked - maxima[..., None]), 0.0)
    totals = jnp.sum(weights, axis=-1)
    outputs = jnp.einsum(out_form, rounded(weights), value_block.astype(jnp.float32))
    return outputs, maxima, totals


def partial_grads(scores, allowed, log_norms, gradient_dot_scores, grad_block, query_block, key_block, value_block, einsum_forms, score_scale):
    score_form, out_form, back_form = einsum_forms
    masked = jnp.where(allowed, scores, negative_fill)
    weights = jnp.where(allowed, jnp.exp(masked - log_norms[..., None]), 0.0)
    grad_float = grad_block.astype(jnp.float32)
    grad_values = jnp.einsum(back_form, rounded(weights), grad_float)
    grad_weights = jnp.einsum(score_form, grad_float, value_block.astype(jnp.float32))
    grad_scores = rounded(weights * (grad_weights - gradient_dot_scores[..., None]))
    grad_queries = jnp.einsum(out_form, grad_scores, key_block.astype(jnp.float32)) * score_scale
    grad_keys = jnp.einsum(back_form, grad_scores, query_block.astype(jnp.float32)) * score_scale
    return grad_queries, grad_keys, grad_values


def reference(queries, key_vectors, value_vectors, out_weight, attn_grad, tile_column_mask):
    head_count = D // HEAD_DIM
    score_scale = HEAD_DIM ** -0.5
    grid_shape = (ROWS, COLS, head_count, HEAD_DIM)
    query_grid = queries.reshape(grid_shape)
    key_grid = key_vectors.reshape(grid_shape)
    value_grid = value_vectors.reshape(grid_shape)
    grad_grid = attn_grad.reshape(grid_shape)
    causal_row = lax.broadcasted_iota(jnp.int32, (COLS, COLS), 1) <= lax.broadcasted_iota(jnp.int32, (COLS, COLS), 0)
    row_forms = ("qhd,khd->hqk", "hqk,khd->qhd", "hqk,qhd->khd")
    col_forms = ("qchd,kchd->chqk", "chqk,kchd->qchd", "chqk,qchd->kchd")

    def row_logit_scores(query_row, key_row):
        return jnp.einsum(row_forms[0], query_row.astype(jnp.float32), key_row.astype(jnp.float32)) * score_scale

    def row_forward(pieces):
        query_row, key_row, value_row = pieces
        outputs, maxima, totals = partial_attention(row_logit_scores(query_row, key_row), causal_row, value_row, row_forms[1])
        return outputs, maxima.T, totals.T

    row_out, row_max, row_sum = lax.map(row_forward, (query_grid, key_grid, value_grid))

    block_index = jnp.arange(COLS, dtype=jnp.int32) // TILE
    column_allowed_mask = tile_column_mask[block_index] > 0
    earlier = lax.broadcasted_iota(jnp.int32, (ROWS, ROWS), 1) < lax.broadcasted_iota(jnp.int32, (ROWS, ROWS), 0)
    col_allowed = (column_allowed_mask & earlier[None])[:, None]
    col_scores = jnp.einsum(col_forms[0], query_grid.astype(jnp.float32), key_grid.astype(jnp.float32)) * score_scale
    col_out, col_max, col_sum = partial_attention(col_scores, col_allowed, value_grid, col_forms[1])
    col_max = jnp.transpose(col_max, (2, 0, 1))
    col_sum = jnp.transpose(col_sum, (2, 0, 1))

    merged = jnp.maximum(row_max, col_max)
    row_factor = jnp.exp(row_max - merged)
    col_factor = jnp.exp(col_max - merged)
    denominator = row_sum * row_factor + col_sum * col_factor
    log_norms = merged + jnp.log(denominator)
    attention = ((row_out * row_factor[..., None] + col_out * col_factor[..., None]) / denominator[..., None]).astype(jnp.bfloat16)

    flat = attention.reshape(TOKENS, D)
    group = D // N_TP
    projected = jnp.zeros((TOKENS, D), jnp.float32)
    for index in range(N_TP):
        partial_term = jnp.dot(flat[:, index * group:(index + 1) * group], out_weight[index * group:(index + 1) * group], preferred_element_type=jnp.float32)
        projected = projected + rounded(partial_term)
    projected = projected.astype(jnp.bfloat16)

    gradient_dot_scores = jnp.sum(attention.astype(jnp.float32) * grad_grid.astype(jnp.float32), axis=-1)

    def row_backward(pieces):
        query_row, key_row, value_row, grad_row, log_row, dots_row = pieces
        return partial_grads(row_logit_scores(query_row, key_row), causal_row, log_row.T, dots_row.T, grad_row, query_row, key_row, value_row, row_forms, score_scale)

    row_grad_query, row_grad_key, row_grad_value = lax.map(row_backward, (query_grid, key_grid, value_grid, grad_grid, log_norms, gradient_dot_scores))
    col_grad_query, col_grad_key, col_grad_value = partial_grads(col_scores, col_allowed, jnp.transpose(log_norms, (1, 2, 0)), jnp.transpose(gradient_dot_scores, (1, 2, 0)), grad_grid, query_grid, key_grid, value_grid, col_forms, score_scale)
    grad_queries = (row_grad_query + rounded(col_grad_query)).astype(jnp.bfloat16).reshape(TOKENS, D)
    grad_keys = (row_grad_key + rounded(col_grad_key)).astype(jnp.bfloat16).reshape(TOKENS, D)
    grad_values = (row_grad_value + rounded(col_grad_value)).astype(jnp.bfloat16).reshape(TOKENS, D)
    return (projected, grad_queries, grad_keys, grad_values)
```

```python
import jax
import jax.numpy as jnp
from jax import lax
from jax.experimental import pallas as pl
from jax.experimental.pallas import tpu as pltpu
from jax.sharding import PartitionSpec as P

HEAD_DIM = 128
COLS = 512
TILE = 128
SCALE = HEAD_DIM ** (-0.5)
NEG = -1e30
BLOCK = 256
CSTAT = 64

bf16 = jnp.bfloat16
f32 = jnp.float32


def dot_nt(a, b):
    return lax.dot_general(a, b, (((1,), (1,)), ((), ())), preferred_element_type=f32)


def dot_tn(a, b):
    return lax.dot_general(a, b, (((0,), (0,)), ((), ())), preferred_element_type=f32)


def dot_nn(a, b):
    return jnp.dot(a, b, preferred_element_type=f32)


def head(h):
    return slice(h * HEAD_DIM, (h + 1) * HEAD_DIM)


def lanes_like(rows):
    return lax.broadcasted_iota(jnp.int32, (rows, 128), 1)


def put_pieces(tile, lanes, first, x):
    hi = x.astype(bf16).astype(f32)
    rest = x - hi
    mid = rest.astype(bf16).astype(f32)
    low = rest - mid
    for n, piece in enumerate((hi, mid, low)):
        tile = jnp.where(lanes == first + n, piece, tile)
    return tile


def take_lanes(tile, first):
    return tile[:, first : first + 1] + (tile[:, first + 1 : first + 2] + tile[:, first + 2 : first + 3])


def take_rows(tile, first):
    return tile[first : first + 1] + (tile[first + 1 : first + 2] + tile[first + 2 : first + 3])


def row_forward(q_ref, k_ref, v_ref, g_ref, mask_ref, out_ref, stat_ref, bias_ref, bias_t_ref):
    heads = q_ref.shape[1] // HEAD_DIM
    for start in range(0, COLS, BLOCK):
        rows = slice(start, start + BLOCK)
        keys = slice(0, start + BLOCK)
        allowed = lax.broadcasted_iota(jnp.int32, (BLOCK, start + BLOCK), 1) <= (
            lax.broadcasted_iota(jnp.int32, (BLOCK, start + BLOCK), 0) + start
        )
        lanes = lanes_like(BLOCK)
        tile = jnp.zeros((BLOCK, 128), f32)
        for h in range(heads):
            s = dot_nt(q_ref[rows, head(h)], k_ref[keys, head(h)]) * SCALE
            s = jnp.where(allowed, s, NEG)
            m = jnp.max(s, axis=1, keepdims=True)
            p = jnp.exp(s - m)
            total = jnp.sum(p, axis=1, keepdims=True)
            out = dot_nn(p.astype(bf16), v_ref[keys, head(h)]) / total
            out_ref[rows, head(h)] = out
            dots = jnp.sum(out * g_ref[rows, head(h)].astype(f32), axis=1, keepdims=True)
            tile = put_pieces(tile, lanes, 6 * h, m + jnp.log(total))
            tile = put_pieces(tile, lanes, 6 * h + 3, dots)
        stat_ref[rows, :] = tile.astype(bf16)
    total_rows = mask_ref.shape[0]
    width = COLS // total_rows
    mask = mask_ref[...].astype(f32).astype(bf16)
    spread = (
        lax.broadcasted_iota(jnp.int32, (COLS, total_rows), 0) // width
        == lax.broadcasted_iota(jnp.int32, (COLS, total_rows), 1)
    )
    spread = jnp.where(spread, 1.0, 0.0).astype(bf16)
    first = lax.broadcasted_iota(jnp.int32, (COLS, COLS), 0)
    second = lax.broadcasted_iota(jnp.int32, (COLS, COLS), 1)
    same = (first % width) == (second % width)
    whole = dot_nt(dot_nn(spread, mask).astype(bf16), spread)
    whole_t = dot_nt(spread, dot_nn(spread, mask).astype(bf16))
    bias_ref[...] = jnp.where((whole > 0.5) & same & (second < first), 0.0, NEG)
    bias_t_ref[...] = jnp.where((whole_t > 0.5) & same & (first < second), 0.0, NEG)


def col_forward(y_ref, bias_ref, g_ref, stat_ref, send_ref):
    features = g_ref.shape[1]
    heads = features // HEAD_DIM
    send_ref[:, :features] = g_ref[...]
    for start in range(0, COLS, BLOCK):
        rows = slice(start, start + BLOCK)
        keys = slice(0, start + BLOCK)
        lanes = lanes_like(BLOCK)
        tile = stat_ref[rows, :].astype(f32)
        for h in range(heads):
            q = y_ref[rows, head(h)]
            k = y_ref[keys, head(heads + h)]
            v = y_ref[keys, head(2 * heads + h)]
            s = dot_nt(q, k) * SCALE + bias_ref[rows, keys]
            m = jnp.max(s, axis=1, keepdims=True)
            p = jnp.exp(s - m)
            total = jnp.sum(p, axis=1, keepdims=True)
            out = dot_nn(p.astype(bf16), v) / total
            send_ref[rows, head(heads + h)] = out.astype(bf16)
            tile = put_pieces(tile, lanes, CSTAT + 3 * h, m + jnp.log(total))
        send_ref[rows, 2 * features :] = tile.astype(bf16)


def col_backward(y_ref, got_ref, sent_ref, bias_t_ref, send_ref):
    features = y_ref.shape[1] // 3
    heads = features // HEAD_DIM
    lanes = lanes_like(COLS)
    tile = jnp.where(
        lanes < CSTAT,
        got_ref[:, 2 * features :].astype(f32),
        sent_ref[:, 2 * features :].astype(f32),
    )
    for h in range(heads):
        product = got_ref[:, head(h)].astype(f32) * sent_ref[:, head(heads + h)].astype(f32)
        tile = jnp.where(lanes == 32 + h, jnp.sum(product, axis=1, keepdims=True), tile)
    tile = tile.T
    for h in range(heads):
        row_lse = take_rows(tile, 6 * h)
        row_dots = take_rows(tile, 6 * h + 3)
        col_lse = take_rows(tile, CSTAT + 3 * h)
        col_dots = tile[32 + h : 33 + h]
        top = jnp.maximum(row_lse, col_lse)
        row_factor = jnp.exp(row_lse - top)
        col_factor = jnp.exp(col_lse - top)
        both = row_factor + col_factor
        lse = top + jnp.log(both)
        dots = (row_dots * row_factor + col_dots * col_factor) / both
        gradients(
            lambda at: y_ref[at, head(h)],
            lambda at: y_ref[at, head(heads + h)],
            lambda at: y_ref[at, head(2 * heads + h)],
            lambda at: got_ref[at, head(h)],
            lse,
            dots,
            lambda s, keys, rows: s + bias_t_ref[keys, rows],
            send_ref,
            h,
            heads,
            bf16,
        )


def gradients(q, k, v, g, lse, dots, masked, out_ref, h, heads, kind):
    grad_q = None
    for start in range(COLS - BLOCK, -1, -BLOCK):
        keys = slice(start, start + BLOCK)
        rows = slice(start, COLS)
        s = masked(dot_nt(k(keys), q(rows)) * SCALE, keys, rows)
        p = jnp.exp(s - lse[:, start:])
        d = dot_nt(v(keys), g(rows))
        ds = (p * (d - dots[:, start:])).astype(bf16)
        out_ref[keys, head(2 * heads + h)] = dot_nn(p.astype(bf16), g(rows)).astype(kind)
        out_ref[keys, head(heads + h)] = (dot_nn(ds, q(rows)) * SCALE).astype(kind)
        term = dot_tn(ds, k(keys)) * SCALE
        if grad_q is not None:
            term = term + jnp.concatenate([jnp.zeros((BLOCK, HEAD_DIM), f32), grad_q], axis=0)
        grad_q = term
    out_ref[:, head(h)] = grad_q.astype(kind)


def row_merge(out_ref, stat_ref, got_ref, g_ref, weight_ref, part_ref, merged_ref):
    features = g_ref.shape[1]
    heads = features // HEAD_DIM
    lanes = lanes_like(COLS)
    row_tile = stat_ref[...].astype(f32)
    col_tile = got_ref[:, 2 * features :].astype(f32)
    merged = jnp.zeros((COLS, 128), f32)
    parts = []
    for h in range(heads):
        row_lse = take_lanes(row_tile, 6 * h)
        col_lse = take_lanes(col_tile, CSTAT + 3 * h)
        top = jnp.maximum(row_lse, col_lse)
        row_factor = jnp.exp(row_lse - top)
        col_factor = jnp.exp(col_lse - top)
        both = row_factor + col_factor
        att = (
            out_ref[:, head(h)] * row_factor + got_ref[:, head(heads + h)].astype(f32) * col_factor
        ) / both
        att = att.astype(bf16)
        parts.append(att)
        dots = jnp.sum(att.astype(f32) * g_ref[:, head(h)].astype(f32), axis=1, keepdims=True)
        merged = jnp.where(lanes == 2 * h, top + jnp.log(both), merged)
        merged = jnp.where(lanes == 2 * h + 1, dots, merged)
    merged_ref[...] = merged
    att = jnp.concatenate(parts, axis=1)
    step = 512
    for start in range(0, weight_ref.shape[1], step):
        at = slice(start, start + step)
        part_ref[:, at] = dot_nn(att, weight_ref[:, at]).astype(bf16)


def row_backward(q_ref, k_ref, v_ref, g_ref, merged_ref, grad_ref):
    heads = q_ref.shape[1] // HEAD_DIM
    tile = merged_ref[...].T

    def masked(s, keys, rows):
        allowed = (lax.broadcasted_iota(jnp.int32, s.shape, 0) + keys.start) <= (
            lax.broadcasted_iota(jnp.int32, s.shape, 1) + rows.start
        )
        return jnp.where(allowed, s, NEG)

    for h in range(heads):
        gradients(
            lambda at: q_ref[at, head(h)],
            lambda at: k_ref[at, head(h)],
            lambda at: v_ref[at, head(h)],
            lambda at: g_ref[at, head(h)],
            tile[2 * h : 2 * h + 1],
            tile[2 * h + 1 : 2 * h + 2],
            masked,
            grad_ref,
            h,
            heads,
            f32,
        )


def finish(grad_ref, back_ref, q_ref, k_ref, v_ref):
    features = q_ref.shape[1]
    for n, ref in enumerate((q_ref, k_ref, v_ref)):
        at = slice(n * features, (n + 1) * features)
        ref[...] = (grad_ref[:, at] + back_ref[:, at].astype(f32)).astype(bf16)


def call(kernel, outs, cost, *args):
    spec = pl.BlockSpec(memory_space=pltpu.VMEM)
    flops, exps = cost
    moved = sum(a.size * a.dtype.itemsize for a in args)
    moved += sum(o.size * o.dtype.itemsize for o in outs)
    return pl.pallas_call(
        kernel,
        out_shape=outs,
        in_specs=[spec] * len(args),
        out_specs=[spec] * len(outs),
        cost_estimate=pl.CostEstimate(flops=flops, bytes_accessed=moved, transcendentals=exps),
        compiler_params=pltpu.CompilerParams(vmem_limit_bytes=32 * 1024 * 1024),
        name=kernel.__name__,
    )(*args)


def exchange(x):
    return lax.all_to_all(x, "seq", split_axis=0, concat_axis=0, tiled=True)


def local(queries, key_vectors, value_vectors, out_weight, attn_grad, tile_column_mask):
    tokens, features = queries.shape
    heads = features // HEAD_DIM
    width = COLS // lax.axis_size("seq")
    block = (lax.axis_index("seq") * width) // TILE
    mask = lax.dynamic_index_in_dim(tile_column_mask, block, 0, keepdims=False)
    product = 2 * COLS * COLS * HEAD_DIM * heads
    exps = COLS * COLS * heads

    def arr(columns, kind):
        return jax.ShapeDtypeStruct((tokens, columns), kind)

    qkv = exchange(jnp.concatenate([queries, key_vectors, value_vectors], axis=1))
    row_out, row_stat, bias, bias_t = call(
        row_forward,
        [arr(features, f32), arr(128, bf16), arr(COLS, f32), arr(COLS, f32)],
        (2 * product, exps),
        queries, key_vectors, value_vectors, attn_grad, mask,
    )
    (sent,) = call(
        col_forward,
        [arr(2 * features + 128, bf16)],
        (2 * product, exps),
        qkv, bias, attn_grad, row_stat,
    )
    got = exchange(sent)
    (col_grads,) = call(
        col_backward, [arr(3 * features, bf16)], (5 * product, exps), qkv, got, sent, bias_t
    )
    back = exchange(col_grads)
    part, merged = call(
        row_merge,
        [arr(out_weight.shape[1], bf16), arr(128, f32)],
        (2 * tokens * features * out_weight.shape[1], tokens),
        row_out, row_stat, got, attn_grad, out_weight,
    )
    projected = lax.psum_scatter(part, "tp", scatter_dimension=1, tiled=True)
    (row_grads,) = call(
        row_backward, [arr(3 * features, f32)], (5 * product, exps),
        queries, key_vectors, value_vectors, attn_grad, merged,
    )
    grads = call(finish, [arr(features, bf16)] * 3, (3 * tokens * features, 0), row_grads, back)
    return (projected, *grads)


def solution(mesh):
    return jax.shard_map(
        local,
        mesh=mesh,
        in_specs=(
            P("seq", "tp"),
            P("seq", "tp"),
            P("seq", "tp"),
            P("tp", None),
            P("seq", "tp"),
            P(),
        ),
        out_specs=(P("seq", "tp"), P("seq", "tp"), P("seq", "tp"), P("seq", "tp")),
        check_vma=False,
    )
```

```python
import jax
import jax.numpy as jnp
from jax import lax
from jax.experimental import pallas as pl
from jax.experimental.pallas import tpu as pltpu
from jax.sharding import PartitionSpec as P

HEAD_DIM = 128
COLS = 512
TILE = 128
SCALE = HEAD_DIM ** (-0.5)
NEG = -1e30
BLOCK = 256
CSTAT = 64

bf16 = jnp.bfloat16
f32 = jnp.float32


def dot_nt(a, b):
    return lax.dot_general(a, b, (((1,), (1,)), ((), ())), preferred_element_type=f32)


def dot_tn(a, b):
    return lax.dot_general(a, b, (((0,), (0,)), ((), ())), preferred_element_type=f32)


def dot_nn(a, b):
    return jnp.dot(a, b, preferred_element_type=f32)


def head(h):
    return slice(h * HEAD_DIM, (h + 1) * HEAD_DIM)


def lanes_like(rows):
    return lax.broadcasted_iota(jnp.int32, (rows, 128), 1)


def put_pieces(tile, lanes, first, x):
    hi = x.astype(bf16).astype(f32)
    rest = x - hi
    mid = rest.astype(bf16).astype(f32)
    low = rest - mid
    for n, piece in enumerate((hi, mid, low)):
        tile = jnp.where(lanes == first + n, piece, tile)
    return tile


def take_lanes(tile, first):
    return tile[:, first : first + 1] + (tile[:, first + 1 : first + 2] + tile[:, first + 2 : first + 3])


def take_rows(tile, first):
    return tile[first : first + 1] + (tile[first + 1 : first + 2] + tile[first + 2 : first + 3])


def row_forward(q_ref, k_ref, v_ref, g_ref, mask_ref, out_ref, stat_ref, bias_ref, bias_t_ref):
    heads = q_ref.shape[1] // HEAD_DIM
    for start in range(0, COLS, BLOCK):
        rows = slice(start, start + BLOCK)
        keys = slice(0, start + BLOCK)
        allowed = lax.broadcasted_iota(jnp.int32, (BLOCK, start + BLOCK), 1) <= (
            lax.broadcasted_iota(jnp.int32, (BLOCK, start + BLOCK), 0) + start
        )
        lanes = lanes_like(BLOCK)
        tile = jnp.zeros((BLOCK, 128), f32)
        for h in range(heads):
            s = dot_nt(q_ref[rows, head(h)], k_ref[keys, head(h)]) * SCALE
            s = jnp.where(allowed, s, NEG)
            m = jnp.max(s, axis=1, keepdims=True)
            p = jnp.exp(s - m)
            total = jnp.sum(p, axis=1, keepdims=True)
            out = dot_nn(p.astype(bf16), v_ref[keys, head(h)]) / total
            out_ref[rows, head(h)] = out
            dots = jnp.sum(out * g_ref[rows, head(h)].astype(f32), axis=1, keepdims=True)
            tile = put_pieces(tile, lanes, 6 * h, m + jnp.log(total))
            tile = put_pieces(tile, lanes, 6 * h + 3, dots)
        stat_ref[rows, :] = tile.astype(bf16)
    total_rows = mask_ref.shape[0]
    width = COLS // total_rows
    mask = mask_ref[...].astype(f32).astype(bf16)
    spread = (
        lax.broadcasted_iota(jnp.int32, (COLS, total_rows), 0) // width
        == lax.broadcasted_iota(jnp.int32, (COLS, total_rows), 1)
    )
    spread = jnp.where(spread, 1.0, 0.0).astype(bf16)
    first = lax.broadcasted_iota(jnp.int32, (COLS, COLS), 0)
    second = lax.broadcasted_iota(jnp.int32, (COLS, COLS), 1)
    same = (first % width) == (second % width)
    whole = dot_nt(dot_nn(spread, mask).astype(bf16), spread)
    whole_t = dot_nt(spread, dot_nn(spread, mask).astype(bf16))
    bias_ref[...] = jnp.where((whole > 0.5) & same & (second < first), 0.0, NEG).astype(bf16)
    bias_t_ref[...] = jnp.where((whole_t > 0.5) & same & (first < second), 0.0, NEG).astype(bf16)


def col_forward_joined(key_ref, rest_ref, bias_ref, g_ref, stat_ref, send_ref, y_ref):
    features = g_ref.shape[1]
    y_ref[:, :features] = rest_ref[:, :features]
    y_ref[:, features : 2 * features] = key_ref[...]
    y_ref[:, 2 * features :] = rest_ref[:, features:]
    col_forward(y_ref, bias_ref, g_ref, stat_ref, send_ref)


def col_forward(y_ref, bias_ref, g_ref, stat_ref, send_ref):
    features = g_ref.shape[1]
    heads = features // HEAD_DIM
    send_ref[:, :features] = g_ref[...]
    for start in range(0, COLS, BLOCK):
        rows = slice(start, start + BLOCK)
        keys = slice(0, start + BLOCK)
        lanes = lanes_like(BLOCK)
        tile = stat_ref[rows, :].astype(f32)
        for h in range(heads):
            q = y_ref[rows, head(h)]
            k = y_ref[keys, head(heads + h)]
            v = y_ref[keys, head(2 * heads + h)]
            s = dot_nt(q, k) * SCALE + bias_ref[rows, keys].astype(f32)
            m = jnp.max(s, axis=1, keepdims=True)
            p = jnp.exp(s - m)
            total = jnp.sum(p, axis=1, keepdims=True)
            out = dot_nn(p.astype(bf16), v) / total
            send_ref[rows, head(heads + h)] = out.astype(bf16)
            tile = put_pieces(tile, lanes, CSTAT + 3 * h, m + jnp.log(total))
        send_ref[rows, 2 * features :] = tile.astype(bf16)


def col_backward(y_ref, got_ref, sent_ref, bias_t_ref, send_ref):
    features = y_ref.shape[1] // 3
    heads = features // HEAD_DIM
    lanes = lanes_like(COLS)
    tile = jnp.where(
        lanes < CSTAT,
        got_ref[:, 2 * features :].astype(f32),
        sent_ref[:, 2 * features :].astype(f32),
    )
    for h in range(heads):
        product = got_ref[:, head(h)].astype(f32) * sent_ref[:, head(heads + h)].astype(f32)
        tile = jnp.where(lanes == 32 + h, jnp.sum(product, axis=1, keepdims=True), tile)
    tile = tile.T
    for h in range(heads):
        row_lse = take_rows(tile, 6 * h)
        row_dots = take_rows(tile, 6 * h + 3)
        col_lse = take_rows(tile, CSTAT + 3 * h)
        col_dots = tile[32 + h : 33 + h]
        top = jnp.maximum(row_lse, col_lse)
        row_factor = jnp.exp(row_lse - top)
        col_factor = jnp.exp(col_lse - top)
        both = row_factor + col_factor
        lse = top + jnp.log(both)
        dots = (row_dots * row_factor + col_dots * col_factor) / both
        gradients(
            lambda at: y_ref[at, head(h)],
            lambda at: y_ref[at, head(heads + h)],
            lambda at: y_ref[at, head(2 * heads + h)],
            lambda at: got_ref[at, head(h)],
            lse,
            dots,
            lambda s, keys, rows: s + bias_t_ref[keys, rows].astype(f32),
            send_ref,
            h,
            heads,
            bf16,
        )


def gradients(q, k, v, g, lse, dots, masked, out_ref, h, heads, kind):
    grad_q = None
    for start in range(COLS - BLOCK, -1, -BLOCK):
        keys = slice(start, start + BLOCK)
        rows = slice(start, COLS)
        s = masked(dot_nt(k(keys), q(rows)) * SCALE, keys, rows)
        p = jnp.exp(s - lse[:, start:])
        d = dot_nt(v(keys), g(rows))
        ds = (p * (d - dots[:, start:])).astype(bf16)
        out_ref[keys, head(2 * heads + h)] = dot_nn(p.astype(bf16), g(rows)).astype(kind)
        out_ref[keys, head(heads + h)] = (dot_nn(ds, q(rows)) * SCALE).astype(kind)
        term = dot_tn(ds, k(keys)) * SCALE
        if grad_q is not None:
            term = term + jnp.concatenate([jnp.zeros((BLOCK, HEAD_DIM), f32), grad_q], axis=0)
        grad_q = term
    out_ref[:, head(h)] = grad_q.astype(kind)


def row_merge(core_ref, out_ref, stat_ref, got_ref, g_ref, weight_ref, keep_ref, give_ref, merged_ref):
    features = g_ref.shape[1]
    heads = features // HEAD_DIM
    lanes = lanes_like(COLS)
    row_tile = stat_ref[...].astype(f32)
    col_tile = got_ref[:, 2 * features :].astype(f32)
    merged = jnp.zeros((COLS, 128), f32)
    parts = []
    for h in range(heads):
        row_lse = take_lanes(row_tile, 6 * h)
        col_lse = take_lanes(col_tile, CSTAT + 3 * h)
        top = jnp.maximum(row_lse, col_lse)
        row_factor = jnp.exp(row_lse - top)
        col_factor = jnp.exp(col_lse - top)
        both = row_factor + col_factor
        att = (
            out_ref[:, head(h)] * row_factor + got_ref[:, head(heads + h)].astype(f32) * col_factor
        ) / both
        att = att.astype(bf16)
        parts.append(att)
        dots = jnp.sum(att.astype(f32) * g_ref[:, head(h)].astype(f32), axis=1, keepdims=True)
        merged = jnp.where(lanes == 2 * h, top + jnp.log(both), merged)
        merged = jnp.where(lanes == 2 * h + 1, dots, merged)
    merged_ref[...] = merged
    att = jnp.concatenate(parts, axis=1)
    core = core_ref[0]
    for n in range(weight_ref.shape[1] // (2 * features)):
        for ref, side in ((keep_ref, core), (give_ref, 1 - core)):
            at = pl.ds(pl.multiple_of((2 * n + side) * features, 128), features)
            ref[:, n * features : (n + 1) * features] = dot_nn(att, weight_ref[:, at]).astype(bf16)


def pair_sum(x_ref, keep_ref, got_ref, own_ref, *send_refs):
    features = own_ref.shape[1]
    count = 1 + len(send_refs)
    for n, ref in enumerate((own_ref, *send_refs)):
        chip = lax.rem(x_ref[0] + n, count)
        at = pl.ds(pl.multiple_of(chip * features, 128), features)
        ref[...] = (keep_ref[:, at].astype(f32) + got_ref[:, at].astype(f32)).astype(ref.dtype)


def row_backward(q_ref, k_ref, v_ref, g_ref, merged_ref, grad_ref):
    heads = q_ref.shape[1] // HEAD_DIM
    tile = merged_ref[...].T

    def masked(s, keys, rows):
        allowed = (lax.broadcasted_iota(jnp.int32, s.shape, 0) + keys.start) <= (
            lax.broadcasted_iota(jnp.int32, s.shape, 1) + rows.start
        )
        return jnp.where(allowed, s, NEG)

    for h in range(heads):
        gradients(
            lambda at: q_ref[at, head(h)],
            lambda at: k_ref[at, head(h)],
            lambda at: v_ref[at, head(h)],
            lambda at: g_ref[at, head(h)],
            tile[2 * h : 2 * h + 1],
            tile[2 * h + 1 : 2 * h + 2],
            masked,
            grad_ref,
            h,
            heads,
            f32,
        )


def finish(grad_ref, back_ref, own_ref, p1_ref, p2_ref, p3_ref, projected_ref, q_ref, k_ref, v_ref):
    features = q_ref.shape[1]
    for n, ref in enumerate((q_ref, k_ref, v_ref)):
        at = slice(n * features, (n + 1) * features)
        ref[...] = (grad_ref[:, at] + back_ref[:, at].astype(f32)).astype(bf16)
    total = own_ref[...]
    for ref in (p1_ref, p2_ref, p3_ref):
        total = total + ref[...].astype(f32)
    projected_ref[...] = total.astype(bf16)


def call(kernel, outs, cost, *args):
    vmem = pl.BlockSpec(memory_space=pltpu.VMEM)
    smem = pl.BlockSpec(memory_space=pltpu.SMEM)
    flops, exps = cost
    moved = sum(a.size * a.dtype.itemsize for a in args)
    moved += sum(o.size * o.dtype.itemsize for o in outs)
    return pl.pallas_call(
        kernel,
        out_shape=outs,
        in_specs=[smem if a.ndim == 1 else vmem for a in args],
        out_specs=[vmem] * len(outs),
        cost_estimate=pl.CostEstimate(flops=flops, bytes_accessed=moved, transcendentals=exps),
        compiler_params=pltpu.CompilerParams(vmem_limit_bytes=16 * 1024 * 1024),
        name=kernel.__name__,
    )(*args)


def exchange(x):
    return lax.all_to_all(x, "seq", split_axis=0, concat_axis=0, tiled=True)


def local(queries, key_vectors, value_vectors, out_weight, attn_grad, tile_column_mask):
    tokens, features = queries.shape
    heads = features // HEAD_DIM
    width = COLS // lax.axis_size("seq")
    block = (lax.axis_index("seq") * width) // TILE
    mask = lax.dynamic_index_in_dim(tile_column_mask, block, 0, keepdims=False)
    product = 2 * COLS * COLS * HEAD_DIM * heads
    exps = COLS * COLS * heads

    def arr(columns, kind):
        return jax.ShapeDtypeStruct((tokens, columns), kind)

    def forward(queries, key_vectors, value_vectors, attn_grad, mask):
        return call(
            row_forward,
            [arr(features, f32), arr(128, bf16), arr(COLS, bf16), arr(COLS, bf16)],
            (2 * product, exps),
            queries, key_vectors, value_vectors, attn_grad, mask,
        )

    def at_once(queries, key_vectors, value_vectors, attn_grad, mask):
        qkv = exchange(jnp.concatenate([queries, key_vectors, value_vectors], axis=1))
        row_out, row_stat, bias, bias_t = forward(queries, key_vectors, value_vectors, attn_grad, mask)
        (sent,) = call(
            col_forward,
            [arr(2 * features + 128, bf16)],
            (2 * product, exps),
            qkv, bias, attn_grad, row_stat,
        )
        return qkv, sent, row_out, row_stat, bias_t

    def in_two(queries, key_vectors, value_vectors, attn_grad, mask):
        keys = exchange(key_vectors)
        row_out, row_stat, bias, bias_t = forward(queries, key_vectors, value_vectors, attn_grad, mask)
        rest, keys = lax.optimization_barrier((jnp.concatenate([queries, value_vectors], axis=1), keys))
        rest = exchange(rest)
        sent, qkv = call(
            col_forward_joined,
            [arr(2 * features + 128, bf16), arr(3 * features, bf16)],
            (2 * product, exps),
            keys, rest, bias, attn_grad, row_stat,
        )
        return qkv, sent, row_out, row_stat, bias_t

    place = lax.axis_index("tp")
    core = lax.rem(place, 2)
    qkv, sent, row_out, row_stat, bias_t = lax.cond(
        core == 1, in_two, at_once, queries, key_vectors, value_vectors, attn_grad, mask
    )
    got = exchange(sent)
    (col_grads,) = call(
        col_backward, [arr(3 * features, bf16)], (5 * product, exps), qkv, got, sent, bias_t
    )
    back = exchange(col_grads)
    got, col_grads = lax.optimization_barrier((got, col_grads))
    half = out_weight.shape[1] // 2
    keep, give, merged = call(
        row_merge,
        [arr(half, bf16), arr(half, bf16), arr(128, f32)],
        (2 * tokens * features * out_weight.shape[1], tokens),
        core.reshape(1), row_out, row_stat, got, attn_grad, out_weight,
    )
    count = lax.axis_size("tp")
    chips = count // 2
    pair = lax.ppermute(give, "tp", [(t, t ^ 1) for t in range(count)])
    own, *sends = call(
        pair_sum,
        [arr(features, f32)] + [arr(features, bf16)] * (chips - 1),
        (tokens * half, 0),
        (place // 2).reshape(1), keep, pair,
    )
    parts = [
        lax.ppermute(x, "tp", [(t, (t + 2 * n) % count) for t in range(count)])
        for n, x in enumerate(sends, 1)
    ]
    (row_grads,) = call(
        row_backward, [arr(3 * features, f32)], (5 * product, exps),
        queries, key_vectors, value_vectors, attn_grad, merged,
    )
    return tuple(
        call(finish, [arr(features, bf16)] * 4, (6 * tokens * features, 0), row_grads, back, own, *parts)
    )


def solution(mesh):
    return jax.shard_map(
        local,
        mesh=mesh,
        in_specs=(
            P("seq", "tp"),
            P("seq", "tp"),
            P("seq", "tp"),
            P("tp", None),
            P("seq", "tp"),
            P(),
        ),
        out_specs=(P("seq", "tp"), P("seq", "tp"), P("seq", "tp"), P("seq", "tp")),
        check_vma=False,
    )
```

```python
import jax
import jax.numpy as jnp
from jax import lax
from jax.experimental import pallas as pl
from jax.experimental.pallas import tpu as pltpu
from jax.sharding import PartitionSpec as P

HEAD_DIM = 128
COLS = 512
TILE = 128
SCALE = HEAD_DIM ** (-0.5)
NEG = -1e30
BLOCK = 256
CSTAT = 64

bf16 = jnp.bfloat16
f32 = jnp.float32


def dot_nt(a, b):
    return lax.dot_general(a, b, (((1,), (1,)), ((), ())), preferred_element_type=f32)


def dot_tn(a, b):
    return lax.dot_general(a, b, (((0,), (0,)), ((), ())), preferred_element_type=f32)


def dot_nn(a, b):
    return jnp.dot(a, b, preferred_element_type=f32)


def head(h):
    return slice(h * HEAD_DIM, (h + 1) * HEAD_DIM)


def lanes_like(rows):
    return lax.broadcasted_iota(jnp.int32, (rows, 128), 1)


def put_pieces(tile, lanes, first, x):
    hi = x.astype(bf16).astype(f32)
    rest = x - hi
    mid = rest.astype(bf16).astype(f32)
    low = rest - mid
    for n, piece in enumerate((hi, mid, low)):
        tile = jnp.where(lanes == first + n, piece, tile)
    return tile


def take_lanes(tile, first):
    return tile[:, first : first + 1] + (tile[:, first + 1 : first + 2] + tile[:, first + 2 : first + 3])


def take_rows(tile, first):
    return tile[first : first + 1] + (tile[first + 1 : first + 2] + tile[first + 2 : first + 3])


def row_forward(q_ref, k_ref, v_ref, g_ref, mask_ref, out_ref, stat_ref, bias_ref):
    heads = q_ref.shape[1] // HEAD_DIM
    for start in range(0, COLS, BLOCK):
        rows = slice(start, start + BLOCK)
        keys = slice(0, start + BLOCK)
        allowed = lax.broadcasted_iota(jnp.int32, (BLOCK, start + BLOCK), 1) <= (
            lax.broadcasted_iota(jnp.int32, (BLOCK, start + BLOCK), 0) + start
        )
        lanes = lanes_like(BLOCK)
        tile = jnp.zeros((BLOCK, 128), f32)
        for h in range(heads):
            s = dot_nt(q_ref[rows, head(h)], k_ref[keys, head(h)]) * SCALE
            s = jnp.where(allowed, s, NEG)
            m = jnp.max(s, axis=1, keepdims=True)
            p = jnp.exp(s - m)
            total = jnp.sum(p, axis=1, keepdims=True)
            out = dot_nn(p.astype(bf16), v_ref[keys, head(h)]) / total
            out_ref[rows, head(h)] = out
            dots = jnp.sum(out * g_ref[rows, head(h)].astype(f32), axis=1, keepdims=True)
            tile = put_pieces(tile, lanes, 6 * h, m + jnp.log(total))
            tile = put_pieces(tile, lanes, 6 * h + 3, dots)
        stat_ref[rows, :] = tile.astype(bf16)
    pattern(mask_ref, bias_ref)


def pattern(mask_ref, bias_ref, turned=False):
    total_rows = mask_ref.shape[0]
    width = COLS // total_rows
    mask = mask_ref[...].astype(f32).astype(bf16)
    spread = (
        lax.broadcasted_iota(jnp.int32, (COLS, total_rows), 0) // width
        == lax.broadcasted_iota(jnp.int32, (COLS, total_rows), 1)
    )
    spread = jnp.where(spread, 1.0, 0.0).astype(bf16)
    query = lax.broadcasted_iota(jnp.int32, (COLS, COLS), int(turned))
    key = lax.broadcasted_iota(jnp.int32, (COLS, COLS), 1 - int(turned))
    same = (query % width) == (key % width)
    rows = dot_nn(spread, mask).astype(bf16)
    whole = dot_nt(spread, rows) if turned else dot_nt(rows, spread)
    bias_ref[...] = jnp.where((whole > 0.5) & same & (key < query), 0.0, NEG).astype(bf16)


def pattern_turned(mask_ref, *refs):
    *_, bias_ref = refs
    pattern(mask_ref, bias_ref, turned=True)


def pack(pieces, refs):
    *ins, out_ref, sems = refs
    copies = []
    at = 0
    for n, (ref, (first, width)) in enumerate(zip(ins, pieces)):
        copies.append(
            pltpu.make_async_copy(
                ref.at[:, first : first + width], out_ref.at[:, at : at + width], sems.at[n]
            )
        )
        at += width
    for copy in copies:
        copy.start()
    for copy in copies:
        copy.wait()


def col_forward_joined(first_ref, rest_ref, bias_ref, g_ref, stat_ref, send_ref, y_ref):
    features = g_ref.shape[1]
    y_ref[:, :features] = rest_ref[:, :features]
    y_ref[:, features : features + HEAD_DIM] = first_ref[...]
    y_ref[:, features + HEAD_DIM :] = rest_ref[:, features:]
    col_forward(y_ref, bias_ref, g_ref, stat_ref, send_ref)


def col_forward(y_ref, bias_ref, g_ref, stat_ref, send_ref):
    features = g_ref.shape[1]
    heads = features // HEAD_DIM
    send_ref[:, :features] = g_ref[...]
    for start in range(0, COLS, BLOCK):
        rows = slice(start, start + BLOCK)
        keys = slice(0, start + BLOCK)
        lanes = lanes_like(BLOCK)
        tile = jnp.zeros((BLOCK, 128), f32)
        for h in range(heads):
            q = y_ref[rows, head(h)]
            k = y_ref[keys, head(heads + h)]
            v = y_ref[keys, head(2 * heads + h)]
            s = dot_nt(q, k) * SCALE + bias_ref[rows, keys].astype(f32)
            m = jnp.max(s, axis=1, keepdims=True)
            p = jnp.exp(s - m)
            total = jnp.sum(p, axis=1, keepdims=True)
            out = dot_nn(p.astype(bf16), v) / total
            send_ref[rows, head(heads + h)] = out.astype(bf16)
            tile = put_pieces(tile, lanes, CSTAT + 3 * h, m + jnp.log(total))
        tile = jnp.where(lanes < CSTAT, stat_ref[rows, :].astype(f32), tile)
        send_ref[rows, 2 * features :] = tile.astype(bf16)


def col_backward(y_ref, got_ref, sent_ref, bias_t_ref, send_ref):
    features = y_ref.shape[1] // 3
    heads = features // HEAD_DIM
    lanes = lanes_like(COLS)
    tile = jnp.where(
        lanes < CSTAT,
        got_ref[:, 2 * features :].astype(f32),
        sent_ref[:, 2 * features :].astype(f32),
    )
    for h in range(heads):
        product = got_ref[:, head(h)].astype(f32) * sent_ref[:, head(heads + h)].astype(f32)
        tile = jnp.where(lanes == 32 + h, jnp.sum(product, axis=1, keepdims=True), tile)
    tile = tile.T
    for h in range(heads):
        row_lse = take_rows(tile, 6 * h)
        row_dots = take_rows(tile, 6 * h + 3)
        col_lse = take_rows(tile, CSTAT + 3 * h)
        col_dots = tile[32 + h : 33 + h]
        top = jnp.maximum(row_lse, col_lse)
        row_factor = jnp.exp(row_lse - top)
        col_factor = jnp.exp(col_lse - top)
        both = row_factor + col_factor
        lse = top + jnp.log(both)
        dots = (row_dots * row_factor + col_dots * col_factor) / both
        gradients(
            lambda at: y_ref[at, head(h)],
            lambda at: y_ref[at, head(heads + h)],
            lambda at: y_ref[at, head(2 * heads + h)],
            lambda at: got_ref[at, head(h)],
            lse,
            dots,
            lambda s, keys, rows: s + bias_t_ref[keys, rows].astype(f32),
            send_ref,
            h,
            heads,
            bf16,
        )


def gradients(q, k, v, g, lse, dots, masked, out_ref, h, heads, kind):
    grad_q = None
    for start in range(COLS - BLOCK, -1, -BLOCK):
        keys = slice(start, start + BLOCK)
        rows = slice(start, COLS)
        s = masked(dot_nt(k(keys), q(rows)) * SCALE, keys, rows)
        p = jnp.exp(s - lse[:, start:])
        d = dot_nt(v(keys), g(rows))
        ds = (p * (d - dots[:, start:])).astype(bf16)
        out_ref[keys, head(2 * heads + h)] = dot_nn(p.astype(bf16), g(rows)).astype(kind)
        out_ref[keys, head(heads + h)] = (dot_nn(ds, q(rows)) * SCALE).astype(kind)
        term = dot_tn(ds, k(keys)) * SCALE
        if grad_q is not None:
            term = term + jnp.concatenate([jnp.zeros((BLOCK, HEAD_DIM), f32), grad_q], axis=0)
        grad_q = term
    out_ref[:, head(h)] = grad_q.astype(kind)


def row_merge(core_ref, out_ref, sent_ref, got_ref, g_ref, weight_ref, att_ref, give_ref, merged_ref):
    features = g_ref.shape[1]
    heads = features // HEAD_DIM
    lanes = lanes_like(COLS)
    col_tile = got_ref[:, 2 * features :].astype(f32)
    merged = jnp.zeros((COLS, 128), f32)
    parts = []
    row_tile = sent_ref[:, 2 * features :].astype(f32)
    for h in range(heads):
        row_lse = take_lanes(row_tile, 6 * h)
        col_lse = take_lanes(col_tile, CSTAT + 3 * h)
        top = jnp.maximum(row_lse, col_lse)
        row_factor = jnp.exp(row_lse - top)
        col_factor = jnp.exp(col_lse - top)
        both = row_factor + col_factor
        att = (
            out_ref[:, head(h)] * row_factor + got_ref[:, head(heads + h)].astype(f32) * col_factor
        ) / both
        att = att.astype(bf16)
        parts.append(att)
        dots = jnp.sum(att.astype(f32) * g_ref[:, head(h)].astype(f32), axis=1, keepdims=True)
        merged = jnp.where(lanes == 2 * h, top + jnp.log(both), merged)
        merged = jnp.where(lanes == 2 * h + 1, dots, merged)
    merged_ref[...] = merged
    att_ref[...] = jnp.concatenate(parts, axis=1)
    project(1 - core_ref[0], att_ref, weight_ref, give_ref)


def project(core, att_ref, weight_ref, part_ref):
    features = att_ref.shape[1]
    for n in range(weight_ref.shape[1] // (2 * features)):
        at = pl.ds(pl.multiple_of((2 * n + core) * features, 128), features)
        part_ref[:, n * features : (n + 1) * features] = dot_nn(att_ref[...], weight_ref[:, at]).astype(bf16)


def project_own(core_ref, att_ref, weight_ref, part_ref):
    project(core_ref[0], att_ref, weight_ref, part_ref)


def pair_sum(x_ref, keep_ref, got_ref, own_ref, *send_refs):
    features = own_ref.shape[1]
    count = 1 + len(send_refs)
    for n, ref in enumerate((own_ref, *send_refs)):
        chip = lax.rem(x_ref[0] + n, count)
        at = pl.ds(pl.multiple_of(chip * features, 128), features)
        ref[...] = (keep_ref[:, at].astype(f32) + got_ref[:, at].astype(f32)).astype(ref.dtype)


def project_sum(own_ref, *refs):
    *part_refs, out_ref = refs
    total = own_ref[...]
    for ref in part_refs:
        total = total + ref[...].astype(f32)
    out_ref[...] = total.astype(bf16)


def row_backward(q_ref, k_ref, v_ref, g_ref, merged_ref, grad_ref):
    heads = q_ref.shape[1] // HEAD_DIM
    tile = merged_ref[...].T

    def masked(s, keys, rows):
        allowed = (lax.broadcasted_iota(jnp.int32, s.shape, 0) + keys.start) <= (
            lax.broadcasted_iota(jnp.int32, s.shape, 1) + rows.start
        )
        return jnp.where(allowed, s, NEG)

    for h in range(heads):
        gradients(
            lambda at: q_ref[at, head(h)],
            lambda at: k_ref[at, head(h)],
            lambda at: v_ref[at, head(h)],
            lambda at: g_ref[at, head(h)],
            tile[2 * h : 2 * h + 1],
            tile[2 * h + 1 : 2 * h + 2],
            masked,
            grad_ref,
            h,
            heads,
            f32,
        )


def finish(grad_ref, back_ref, q_ref, k_ref, v_ref):
    features = q_ref.shape[1]
    for n, ref in enumerate((q_ref, k_ref, v_ref)):
        at = slice(n * features, (n + 1) * features)
        ref[...] = (grad_ref[:, at] + back_ref[:, at].astype(f32)).astype(bf16)


def call(kernel, outs, cost, *args, far=(), far_out=(), scratch=(), room=16):
    vmem = pl.BlockSpec(memory_space=pltpu.VMEM)
    smem = pl.BlockSpec(memory_space=pltpu.SMEM)
    hbm = pl.BlockSpec(memory_space=pltpu.HBM)
    flops, exps = cost
    moved = sum(a.size * a.dtype.itemsize for a in args)
    moved += sum(o.size * o.dtype.itemsize for o in outs)
    return pl.pallas_call(
        kernel,
        out_shape=outs,
        in_specs=[smem if a.ndim == 1 else hbm if n in far else vmem for n, a in enumerate(args)],
        out_specs=[hbm if n in far_out else vmem for n in range(len(outs))],
        scratch_shapes=scratch,
        cost_estimate=pl.CostEstimate(flops=flops, bytes_accessed=moved, transcendentals=exps),
        compiler_params=pltpu.CompilerParams(vmem_limit_bytes=room * 1024 * 1024),
        name=getattr(kernel, "__name__", "pack"),
    )(*args)


def exchange(x):
    return lax.all_to_all(x, "seq", split_axis=0, concat_axis=0, tiled=True)


def local(queries, key_vectors, value_vectors, out_weight, attn_grad, tile_column_mask):
    tokens, features = queries.shape
    heads = features // HEAD_DIM
    width = COLS // lax.axis_size("seq")
    block = (lax.axis_index("seq") * width) // TILE
    mask = lax.dynamic_index_in_dim(tile_column_mask, block, 0, keepdims=False)
    product = 2 * COLS * COLS * HEAD_DIM * heads
    exps = COLS * COLS * heads

    def arr(columns, kind):
        return jax.ShapeDtypeStruct((tokens, columns), kind)

    def forward(queries, key_vectors, value_vectors, attn_grad, mask):
        return call(
            row_forward,
            [arr(features, f32), arr(128, bf16), arr(COLS, bf16)],
            (2 * product, exps),
            queries, key_vectors, value_vectors, attn_grad, mask,
        )


    def packed(*pieces):
        def kernel(*refs):
            pack([p[1:] for p in pieces], refs)

        return call(
            kernel,
            [arr(sum(p[2] for p in pieces), bf16)],
            (0, 0),
            *[p[0] for p in pieces],
            far=range(len(pieces)),
            scratch=[pltpu.SemaphoreType.DMA((len(pieces),))],
        )[0]

    def at_once(queries, key_vectors, value_vectors, attn_grad, mask):
        qkv = exchange(
            packed((queries, 0, features), (key_vectors, 0, features), (value_vectors, 0, features))
        )
        row_out, row_stat, bias = forward(queries, key_vectors, value_vectors, attn_grad, mask)
        (sent,) = call(
            col_forward,
            [arr(2 * features + 128, bf16)],
            (2 * product, exps),
            qkv, bias, attn_grad, row_stat,
        )
        return qkv, sent, row_out

    def in_two(queries, key_vectors, value_vectors, attn_grad, mask):
        first = exchange(packed((key_vectors, 0, HEAD_DIM)))
        row_out, row_stat, bias = forward(queries, key_vectors, value_vectors, attn_grad, mask)
        rest = packed(
            (queries, 0, features),
            (key_vectors, HEAD_DIM, features - HEAD_DIM),
            (value_vectors, 0, features),
        )
        rest, first = lax.optimization_barrier((rest, first))
        rest = exchange(rest)
        sent, qkv = call(
            col_forward_joined,
            [arr(2 * features + 128, bf16), arr(3 * features, bf16)],
            (2 * product, exps),
            first, rest, bias, attn_grad, row_stat,
        )
        return qkv, sent, row_out

    place = lax.axis_index("tp")
    core = lax.rem(place, 2)
    qkv, sent, row_out = lax.cond(
        core == 1, in_two, at_once, queries, key_vectors, value_vectors, attn_grad, mask
    )
    got = exchange(sent)
    (bias_t,) = call(pattern_turned, [arr(COLS, bf16)], (2 * tokens * tokens * 64, 0), mask, out_weight, row_out, qkv, sent)
    (col_grads,) = call(
        col_backward, [arr(3 * features, bf16)], (5 * product, exps), qkv, got, sent, bias_t
    )
    back = exchange(col_grads)
    got, col_grads = lax.optimization_barrier((got, col_grads))
    half = out_weight.shape[1] // 2
    att, give, merged = call(
        row_merge,
        [arr(features, bf16), arr(half, bf16), arr(128, f32)],
        (2 * tokens * features * half, tokens),
        core.reshape(1), row_out, sent, got, attn_grad, out_weight,
    )
    count = lax.axis_size("tp")
    chips = count // 2
    pair = lax.ppermute(give, "tp", [(t, t ^ 1) for t in range(count)])
    (keep,) = call(
        project_own, [arr(half, bf16)], (2 * tokens * features * half, 0), core.reshape(1), att, out_weight
    )
    own, *sends = call(
        pair_sum,
        [arr(features, f32)] + [arr(features, bf16)] * (chips - 1),
        (tokens * half, 0),
        (place // 2).reshape(1), keep, pair,
    )
    far_first = sorted(range(1, chips), key=lambda n: -min(n, chips - n))
    parts = [
        lax.ppermute(sends[n - 1], "tp", [(t, (t + 2 * n) % count) for t in range(count)])
        for n in far_first
    ]
    (row_grads,) = call(
        row_backward, [arr(3 * features, f32)], (5 * product, exps),
        queries, key_vectors, value_vectors, attn_grad, merged,
    )
    (projected,) = call(project_sum, [arr(features, bf16)], (4 * tokens * features, 0), own, *parts)
    grads = call(finish, [arr(features, bf16)] * 3, (3 * tokens * features, 0), row_grads, back)
    return (projected, *grads)


def solution(mesh):
    return jax.shard_map(
        local,
        mesh=mesh,
        in_specs=(
            P("seq", "tp"),
            P("seq", "tp"),
            P("seq", "tp"),
            P("tp", None),
            P("seq", "tp"),
            P(),
        ),
        out_specs=(P("seq", "tp"), P("seq", "tp"), P("seq", "tp"), P("seq", "tp")),
        check_vma=False,
    )
```

```python
import jax
import jax.numpy as jnp
from jax import lax
from jax.experimental import pallas as pl
from jax.experimental.pallas import tpu as pltpu
from jax.sharding import PartitionSpec as P

HEAD_DIM = 128
COLS = 512
TILE = 128
SCALE = HEAD_DIM ** (-0.5)
NEG = -1e30
BLOCK = 256
CSTAT = 64

bf16 = jnp.bfloat16
f32 = jnp.float32


def dot_nt(a, b):
    return lax.dot_general(a, b, (((1,), (1,)), ((), ())), preferred_element_type=f32)


def dot_tn(a, b):
    return lax.dot_general(a, b, (((0,), (0,)), ((), ())), preferred_element_type=f32)


def dot_nn(a, b):
    return jnp.dot(a, b, preferred_element_type=f32)


def head(h):
    return slice(h * HEAD_DIM, (h + 1) * HEAD_DIM)


def lanes_like(rows):
    return lax.broadcasted_iota(jnp.int32, (rows, 128), 1)


def put_pieces(tile, lanes, first, x):
    hi = x.astype(bf16).astype(f32)
    rest = x - hi
    mid = rest.astype(bf16).astype(f32)
    low = rest - mid
    for n, piece in enumerate((hi, mid, low)):
        tile = jnp.where(lanes == first + n, piece, tile)
    return tile


def take_lanes(tile, first):
    return tile[:, first : first + 1] + (tile[:, first + 1 : first + 2] + tile[:, first + 2 : first + 3])


def take_rows(tile, first):
    return tile[first : first + 1] + (tile[first + 1 : first + 2] + tile[first + 2 : first + 3])


def row_forward(q_ref, k_ref, v_ref, g_ref, mask_ref, out_ref, stat_ref, bias_ref, bias_t_ref):
    heads = q_ref.shape[1] // HEAD_DIM
    for start in range(0, COLS, BLOCK):
        rows = slice(start, start + BLOCK)
        keys = slice(0, start + BLOCK)
        allowed = lax.broadcasted_iota(jnp.int32, (BLOCK, start + BLOCK), 1) <= (
            lax.broadcasted_iota(jnp.int32, (BLOCK, start + BLOCK), 0) + start
        )
        lanes = lanes_like(BLOCK)
        tile = jnp.zeros((BLOCK, 128), f32)
        for h in range(heads):
            s = dot_nt(q_ref[rows, head(h)], k_ref[keys, head(h)]) * SCALE
            s = jnp.where(allowed, s, NEG)
            m = jnp.max(s, axis=1, keepdims=True)
            p = jnp.exp(s - m)
            total = jnp.sum(p, axis=1, keepdims=True)
            out = dot_nn(p.astype(bf16), v_ref[keys, head(h)]) / total
            out_ref[rows, head(h)] = out
            dots = jnp.sum(out * g_ref[rows, head(h)].astype(f32), axis=1, keepdims=True)
            tile = put_pieces(tile, lanes, 6 * h, m + jnp.log(total))
            tile = put_pieces(tile, lanes, 6 * h + 3, dots)
        stat_ref[rows, :] = tile.astype(bf16)
    pattern(mask_ref, bias_ref)
    pattern(mask_ref, bias_t_ref, turned=True)


def pattern(mask_ref, bias_ref, turned=False):
    total_rows = mask_ref.shape[0]
    width = COLS // total_rows
    mask = mask_ref[...].astype(f32).astype(bf16)
    spread = (
        lax.broadcasted_iota(jnp.int32, (COLS, total_rows), 0) // width
        == lax.broadcasted_iota(jnp.int32, (COLS, total_rows), 1)
    )
    spread = jnp.where(spread, 1.0, 0.0).astype(bf16)
    query = lax.broadcasted_iota(jnp.int32, (COLS, COLS), int(turned))
    key = lax.broadcasted_iota(jnp.int32, (COLS, COLS), 1 - int(turned))
    same = (query % width) == (key % width)
    rows = dot_nn(spread, mask).astype(bf16)
    whole = dot_nt(spread, rows) if turned else dot_nt(rows, spread)
    bias_ref[...] = jnp.where((whole > 0.5) & same & (key < query), 0.0, NEG).astype(bf16)


def pack(pieces, refs):
    *ins, out_ref, sems = refs
    copies = []
    at = 0
    for n, (ref, (first, width)) in enumerate(zip(ins, pieces)):
        copies.append(
            pltpu.make_async_copy(
                ref.at[:, first : first + width], out_ref.at[:, at : at + width], sems.at[n]
            )
        )
        at += width
    for copy in copies:
        copy.start()
    for copy in copies:
        copy.wait()


def col_forward_joined(first_ref, rest_ref, bias_ref, g_ref, stat_ref, send_ref, y_ref):
    features = g_ref.shape[1]
    y_ref[:, :features] = rest_ref[:, :features]
    y_ref[:, features : 2 * features] = first_ref[...]
    y_ref[:, 2 * features :] = rest_ref[:, features:]
    col_forward(y_ref, bias_ref, g_ref, stat_ref, send_ref)


def col_forward(y_ref, bias_ref, g_ref, stat_ref, send_ref):
    features = g_ref.shape[1]
    heads = features // HEAD_DIM
    send_ref[:, :features] = g_ref[...]
    for start in range(0, COLS, BLOCK):
        rows = slice(start, start + BLOCK)
        keys = slice(0, start + BLOCK)
        lanes = lanes_like(BLOCK)
        tile = jnp.zeros((BLOCK, 128), f32)
        for h in range(heads):
            q = y_ref[rows, head(h)]
            k = y_ref[keys, head(heads + h)]
            v = y_ref[keys, head(2 * heads + h)]
            s = dot_nt(q, k) * SCALE + bias_ref[rows, keys].astype(f32)
            m = jnp.max(s, axis=1, keepdims=True)
            p = jnp.exp(s - m)
            total = jnp.sum(p, axis=1, keepdims=True)
            out = dot_nn(p.astype(bf16), v) / total
            send_ref[rows, head(heads + h)] = out.astype(bf16)
            tile = put_pieces(tile, lanes, CSTAT + 3 * h, m + jnp.log(total))
        tile = jnp.where(lanes < CSTAT, stat_ref[rows, :].astype(f32), tile)
        send_ref[rows, 2 * features :] = tile.astype(bf16)


def col_backward(y_ref, got_ref, sent_ref, bias_hbm, send_hbm, bias_t_ref, send_ref, sems):
    fetch = pltpu.make_async_copy(bias_hbm, bias_t_ref, sems.at[0])
    fetch.start()
    stores = []
    features = y_ref.shape[1] // 3
    heads = features // HEAD_DIM
    lanes = lanes_like(COLS)
    tile = jnp.where(
        lanes < CSTAT,
        got_ref[:, 2 * features :].astype(f32),
        sent_ref[:, 2 * features :].astype(f32),
    )
    for h in range(heads):
        product = got_ref[:, head(h)].astype(f32) * sent_ref[:, head(heads + h)].astype(f32)
        tile = jnp.where(lanes == 32 + h, jnp.sum(product, axis=1, keepdims=True), tile)
    tile = tile.T
    for h in range(heads):
        row_lse = take_rows(tile, 6 * h)
        row_dots = take_rows(tile, 6 * h + 3)
        col_lse = take_rows(tile, CSTAT + 3 * h)
        col_dots = tile[32 + h : 33 + h]
        top = jnp.maximum(row_lse, col_lse)
        row_factor = jnp.exp(row_lse - top)
        col_factor = jnp.exp(col_lse - top)
        both = row_factor + col_factor
        lse = top + jnp.log(both)
        dots = (row_dots * row_factor + col_dots * col_factor) / both
        gradients(
            lambda at: y_ref[at, head(h)],
            lambda at: y_ref[at, head(heads + h)],
            lambda at: y_ref[at, head(2 * heads + h)],
            lambda at: got_ref[at, head(h)],
            lse,
            dots,
            lambda s, keys, rows: s + bias_t_ref[keys, rows].astype(f32),
            send_ref,
            h,
            heads,
            bf16,
            fetch if h == 0 else None,
        )
        for n in range(3):
            at = head(n * heads + h)
            stores.append(
                pltpu.make_async_copy(send_ref.at[:, at], send_hbm.at[:, at], sems.at[len(stores) + 1])
            )
            stores[-1].start()
    for copy in stores:
        copy.wait()


def gradients(q, k, v, g, lse, dots, masked, out_ref, h, heads, kind, fetch=None):
    grad_q = None
    for start in range(COLS - BLOCK, -1, -BLOCK):
        keys = slice(start, start + BLOCK)
        rows = slice(start, COLS)
        s = dot_nt(k(keys), q(rows)) * SCALE
        d = dot_nt(v(keys), g(rows))
        if fetch is not None:
            fetch.wait()
            fetch = None
        p = jnp.exp(masked(s, keys, rows) - lse[:, start:])
        ds = (p * (d - dots[:, start:])).astype(bf16)
        out_ref[keys, head(2 * heads + h)] = dot_nn(p.astype(bf16), g(rows)).astype(kind)
        out_ref[keys, head(heads + h)] = (dot_nn(ds, q(rows)) * SCALE).astype(kind)
        term = dot_tn(ds, k(keys)) * SCALE
        if grad_q is not None:
            term = term + jnp.concatenate([jnp.zeros((BLOCK, HEAD_DIM), f32), grad_q], axis=0)
        grad_q = term
    out_ref[:, head(h)] = grad_q.astype(kind)


def row_merge(core_ref, out_ref, sent_ref, got_ref, g_ref, weight_ref, att_ref, give_ref, merged_ref):
    features = g_ref.shape[1]
    heads = features // HEAD_DIM
    lanes = lanes_like(COLS)
    col_tile = got_ref[:, 2 * features :].astype(f32)
    merged = jnp.zeros((COLS, 128), f32)
    parts = []
    row_tile = sent_ref[:, 2 * features :].astype(f32)
    for h in range(heads):
        row_lse = take_lanes(row_tile, 6 * h)
        col_lse = take_lanes(col_tile, CSTAT + 3 * h)
        top = jnp.maximum(row_lse, col_lse)
        row_factor = jnp.exp(row_lse - top)
        col_factor = jnp.exp(col_lse - top)
        both = row_factor + col_factor
        att = (
            out_ref[:, head(h)] * row_factor + got_ref[:, head(heads + h)].astype(f32) * col_factor
        ) / both
        att = att.astype(bf16)
        parts.append(att)
        dots = jnp.sum(att.astype(f32) * g_ref[:, head(h)].astype(f32), axis=1, keepdims=True)
        merged = jnp.where(lanes == 2 * h, top + jnp.log(both), merged)
        merged = jnp.where(lanes == 2 * h + 1, dots, merged)
    merged_ref[...] = merged
    att_ref[...] = jnp.concatenate(parts, axis=1)
    project(1 - core_ref[0], att_ref, weight_ref, give_ref)


def project(core, att_ref, weight_ref, part_ref):
    features = att_ref.shape[1]
    for n in range(weight_ref.shape[1] // (2 * features)):
        at = pl.ds(pl.multiple_of((2 * n + core) * features, 128), features)
        part_ref[:, n * features : (n + 1) * features] = dot_nn(att_ref[...], weight_ref[:, at]).astype(bf16)


def project_own(core_ref, att_ref, weight_ref, part_ref):
    project(core_ref[0], att_ref, weight_ref, part_ref)


def pair_sum(x_ref, keep_ref, got_ref, own_ref, *send_refs):
    features = own_ref.shape[1]
    count = 1 + len(send_refs)
    for n, ref in enumerate((own_ref, *send_refs)):
        chip = lax.rem(x_ref[0] + n, count)
        at = pl.ds(pl.multiple_of(chip * features, 128), features)
        ref[...] = (keep_ref[:, at].astype(f32) + got_ref[:, at].astype(f32)).astype(ref.dtype)


def project_sum(own_ref, *refs):
    *part_refs, out_ref = refs
    total = own_ref[...]
    for ref in part_refs:
        total = total + ref[...].astype(f32)
    out_ref[...] = total.astype(bf16)


def row_backward(q_ref, k_ref, v_ref, g_ref, merged_ref, grad_ref):
    heads = q_ref.shape[1] // HEAD_DIM
    tile = merged_ref[...].T

    def masked(s, keys, rows):
        allowed = (lax.broadcasted_iota(jnp.int32, s.shape, 0) + keys.start) <= (
            lax.broadcasted_iota(jnp.int32, s.shape, 1) + rows.start
        )
        return jnp.where(allowed, s, NEG)

    for h in range(heads):
        gradients(
            lambda at: q_ref[at, head(h)],
            lambda at: k_ref[at, head(h)],
            lambda at: v_ref[at, head(h)],
            lambda at: g_ref[at, head(h)],
            tile[2 * h : 2 * h + 1],
            tile[2 * h + 1 : 2 * h + 2],
            masked,
            grad_ref,
            h,
            heads,
            f32,
        )


def finish(grad_ref, back_ref, q_ref, k_ref, v_ref):
    features = q_ref.shape[1]
    for n, ref in enumerate((q_ref, k_ref, v_ref)):
        at = slice(n * features, (n + 1) * features)
        ref[...] = (grad_ref[:, at] + back_ref[:, at].astype(f32)).astype(bf16)


def call(kernel, outs, cost, *args, far=(), far_out=(), scratch=(), room=16):
    vmem = pl.BlockSpec(memory_space=pltpu.VMEM)
    smem = pl.BlockSpec(memory_space=pltpu.SMEM)
    hbm = pl.BlockSpec(memory_space=pltpu.HBM)
    flops, exps = cost
    moved = sum(a.size * a.dtype.itemsize for a in args)
    moved += sum(o.size * o.dtype.itemsize for o in outs)
    return pl.pallas_call(
        kernel,
        out_shape=outs,
        in_specs=[smem if a.ndim == 1 else hbm if n in far else vmem for n, a in enumerate(args)],
        out_specs=[hbm if n in far_out else vmem for n in range(len(outs))],
        scratch_shapes=scratch,
        cost_estimate=pl.CostEstimate(flops=flops, bytes_accessed=moved, transcendentals=exps),
        compiler_params=pltpu.CompilerParams(vmem_limit_bytes=room * 1024 * 1024),
        name=getattr(kernel, "__name__", "pack"),
    )(*args)


def exchange(x):
    return lax.all_to_all(x, "seq", split_axis=0, concat_axis=0, tiled=True)


def local(queries, key_vectors, value_vectors, out_weight, attn_grad, tile_column_mask):
    tokens, features = queries.shape
    heads = features // HEAD_DIM
    width = COLS // lax.axis_size("seq")
    block = (lax.axis_index("seq") * width) // TILE
    mask = lax.dynamic_index_in_dim(tile_column_mask, block, 0, keepdims=False)
    product = 2 * COLS * COLS * HEAD_DIM * heads
    exps = COLS * COLS * heads

    def arr(columns, kind):
        return jax.ShapeDtypeStruct((tokens, columns), kind)

    def forward(queries, key_vectors, value_vectors, attn_grad, mask):
        return call(
            row_forward,
            [arr(features, f32), arr(128, bf16), arr(COLS, bf16), arr(COLS, bf16)],
            (2 * product, exps),
            queries, key_vectors, value_vectors, attn_grad, mask,
        )


    def packed(*pieces):
        def kernel(*refs):
            pack([p[1:] for p in pieces], refs)

        return call(
            kernel,
            [arr(sum(p[2] for p in pieces), bf16)],
            (0, 0),
            *[p[0] for p in pieces],
            far=range(len(pieces)),
            scratch=[pltpu.SemaphoreType.DMA((len(pieces),))],
        )[0]

    def at_once(queries, key_vectors, value_vectors, attn_grad, mask):
        qkv = exchange(
            packed((queries, 0, features), (key_vectors, 0, features), (value_vectors, 0, features))
        )
        row_out, row_stat, bias, bias_t = forward(queries, key_vectors, value_vectors, attn_grad, mask)
        (sent,) = call(
            col_forward,
            [arr(2 * features + 128, bf16)],
            (2 * product, exps),
            qkv, bias, attn_grad, row_stat,
        )
        return qkv, sent, row_out, bias_t

    def in_two(queries, key_vectors, value_vectors, attn_grad, mask):
        first = exchange(key_vectors)
        row_out, row_stat, bias, bias_t = forward(queries, key_vectors, value_vectors, attn_grad, mask)
        rest = packed(
            (queries, 0, features),
            (value_vectors, 0, features),
        )
        rest, first = lax.optimization_barrier((rest, first))
        rest = exchange(rest)
        sent, qkv = call(
            col_forward_joined,
            [arr(2 * features + 128, bf16), arr(3 * features, bf16)],
            (2 * product, exps),
            first, rest, bias, attn_grad, row_stat,
        )
        return qkv, sent, row_out, bias_t

    place = lax.axis_index("tp")
    core = lax.rem(place, 2)
    qkv, sent, row_out, bias_t = lax.cond(
        core == 1, in_two, at_once, queries, key_vectors, value_vectors, attn_grad, mask
    )
    got = exchange(sent)
    (col_grads,) = call(
        col_backward, [arr(3 * features, bf16)], (5 * product, exps), qkv, got, sent, bias_t,
        far=(3,), far_out=(0,),
        scratch=[
            pltpu.VMEM((COLS, COLS), bf16),
            pltpu.VMEM((tokens, 3 * features), bf16),
            pltpu.SemaphoreType.DMA((1 + 3 * heads,)),
        ],
    )
    back = exchange(col_grads)
    got, col_grads = lax.optimization_barrier((got, col_grads))
    half = out_weight.shape[1] // 2
    att, give, merged = call(
        row_merge,
        [arr(features, bf16), arr(half, bf16), arr(128, f32)],
        (2 * tokens * features * half, tokens),
        core.reshape(1), row_out, sent, got, attn_grad, out_weight,
    )
    count = lax.axis_size("tp")
    chips = count // 2
    pair = lax.ppermute(give, "tp", [(t, t ^ 1) for t in range(count)])
    (keep,) = call(
        project_own, [arr(half, bf16)], (2 * tokens * features * half, 0), core.reshape(1), att, out_weight
    )
    own, *sends = call(
        pair_sum,
        [arr(features, f32)] + [arr(features, bf16)] * (chips - 1),
        (tokens * half, 0),
        (place // 2).reshape(1), keep, pair,
    )
    far_first = sorted(range(1, chips), key=lambda n: -min(n, chips - n))
    parts = [
        lax.ppermute(sends[n - 1], "tp", [(t, (t + 2 * n) % count) for t in range(count)])
        for n in far_first
    ]
    (row_grads,) = call(
        row_backward, [arr(3 * features, f32)], (5 * product, exps),
        queries, key_vectors, value_vectors, attn_grad, merged,
    )
    (projected,) = call(project_sum, [arr(features, bf16)], (4 * tokens * features, 0), own, *parts)
    grads = call(finish, [arr(features, bf16)] * 3, (3 * tokens * features, 0), row_grads, back)
    return (projected, *grads)


def solution(mesh):
    return jax.shard_map(
        local,
        mesh=mesh,
        in_specs=(
            P("seq", "tp"),
            P("seq", "tp"),
            P("seq", "tp"),
            P("tp", None),
            P("seq", "tp"),
            P(),
        ),
        out_specs=(P("seq", "tp"), P("seq", "tp"), P("seq", "tp"), P("seq", "tp")),
        check_vma=False,
    )
```

```python
import jax
import jax.numpy as jnp
from jax import lax
from jax.experimental import pallas as pl
from jax.experimental.pallas import tpu as pltpu
from jax.sharding import PartitionSpec as P

HEAD_DIM = 128
COLS = 512
TILE = 128
SCALE = HEAD_DIM ** (-0.5)
NEG = -1e30
FORWARD_BLOCK = 512
BLOCK = 256
CSTAT = 64

bf16 = jnp.bfloat16
f32 = jnp.float32


def dot_nt(a, b):
    return lax.dot_general(a, b, (((1,), (1,)), ((), ())), preferred_element_type=f32)


def dot_tn(a, b):
    return lax.dot_general(a, b, (((0,), (0,)), ((), ())), preferred_element_type=f32)


def dot_nn(a, b):
    return jnp.dot(a, b, preferred_element_type=f32)


def head(h):
    return slice(h * HEAD_DIM, (h + 1) * HEAD_DIM)


def lanes_like(rows):
    return lax.broadcasted_iota(jnp.int32, (rows, 128), 1)


def put_pieces(tile, lanes, first, x):
    hi = x.astype(bf16).astype(f32)
    rest = x - hi
    mid = rest.astype(bf16).astype(f32)
    low = rest - mid
    for n, piece in enumerate((hi, mid, low)):
        tile = jnp.where(lanes == first + n, piece, tile)
    return tile


def take_lanes(tile, first):
    return tile[:, first : first + 1] + (tile[:, first + 1 : first + 2] + tile[:, first + 2 : first + 3])


def take_rows(tile, first):
    return tile[first : first + 1] + (tile[first + 1 : first + 2] + tile[first + 2 : first + 3])


def row_forward(q_ref, k_ref, v_ref, g_ref, mask_ref, out_ref, stat_ref, bias_ref, bias_t_ref):
    heads = q_ref.shape[1] // HEAD_DIM
    for start in range(0, COLS, FORWARD_BLOCK):
        rows = slice(start, start + FORWARD_BLOCK)
        keys = slice(0, start + FORWARD_BLOCK)
        allowed = lax.broadcasted_iota(jnp.int32, (FORWARD_BLOCK, start + FORWARD_BLOCK), 1) <= (
            lax.broadcasted_iota(jnp.int32, (FORWARD_BLOCK, start + FORWARD_BLOCK), 0) + start
        )
        lanes = lanes_like(FORWARD_BLOCK)
        tile = jnp.zeros((FORWARD_BLOCK, 128), f32)
        for h in range(heads):
            s = dot_nt(q_ref[rows, head(h)], k_ref[keys, head(h)]) * SCALE
            s = jnp.where(allowed, s, NEG)
            m = jnp.max(s, axis=1, keepdims=True)
            p = jnp.exp(s - m)
            total = jnp.sum(p, axis=1, keepdims=True)
            out = dot_nn(p.astype(bf16), v_ref[keys, head(h)]) / total
            out_ref[rows, head(h)] = out
            dots = jnp.sum(out * g_ref[rows, head(h)].astype(f32), axis=1, keepdims=True)
            tile = put_pieces(tile, lanes, 6 * h, m + jnp.log(total))
            tile = put_pieces(tile, lanes, 6 * h + 3, dots)
        stat_ref[rows, :] = tile.astype(bf16)
    pattern(mask_ref, bias_ref)
    pattern(mask_ref, bias_t_ref, turned=True)


def pattern(mask_ref, bias_ref, turned=False):
    total_rows = mask_ref.shape[0]
    width = COLS // total_rows
    mask = mask_ref[...].astype(f32).astype(bf16)
    spread = (
        lax.broadcasted_iota(jnp.int32, (COLS, total_rows), 0) // width
        == lax.broadcasted_iota(jnp.int32, (COLS, total_rows), 1)
    )
    spread = jnp.where(spread, 1.0, 0.0).astype(bf16)
    query = lax.broadcasted_iota(jnp.int32, (COLS, COLS), int(turned))
    key = lax.broadcasted_iota(jnp.int32, (COLS, COLS), 1 - int(turned))
    same = (query % width) == (key % width)
    rows = dot_nn(spread, mask).astype(bf16)
    whole = dot_nt(spread, rows) if turned else dot_nt(rows, spread)
    bias_ref[...] = jnp.where((whole > 0.5) & same & (key < query), 0.0, NEG).astype(bf16)


def pack(pieces, refs):
    *ins, out_ref, sems = refs
    copies = []
    at = 0
    for n, (ref, (first, width)) in enumerate(zip(ins, pieces)):
        copies.append(
            pltpu.make_async_copy(
                ref.at[:, first : first + width], out_ref.at[:, at : at + width], sems.at[n]
            )
        )
        at += width
    for copy in copies:
        copy.start()
    for copy in copies:
        copy.wait()


def col_forward_joined(first_ref, rest_ref, bias_ref, g_ref, stat_ref, send_ref, y_ref):
    features = g_ref.shape[1]
    y_ref[:, :features] = rest_ref[:, :features]
    y_ref[:, features : features + HEAD_DIM] = first_ref[...]
    y_ref[:, features + HEAD_DIM :] = rest_ref[:, features:]
    col_forward(y_ref, bias_ref, g_ref, stat_ref, send_ref)


def col_forward(y_ref, bias_ref, g_ref, stat_ref, send_ref):
    features = g_ref.shape[1]
    heads = features // HEAD_DIM
    send_ref[:, :features] = g_ref[...]
    for start in range(0, COLS, FORWARD_BLOCK):
        rows = slice(start, start + FORWARD_BLOCK)
        keys = slice(0, start + FORWARD_BLOCK)
        lanes = lanes_like(FORWARD_BLOCK)
        tile = jnp.zeros((FORWARD_BLOCK, 128), f32)
        scores = [
            dot_nt(y_ref[rows, head(h)], y_ref[keys, head(heads + h)]) * SCALE
            + bias_ref[rows, keys].astype(f32)
            for h in range(heads)
        ]
        tops = [jnp.max(x, axis=1, keepdims=True) for x in scores]
        weights = [jnp.exp(x - m) for x, m in zip(scores, tops)]
        totals = [jnp.sum(p, axis=1, keepdims=True) for p in weights]
        for h, (m, p, total) in enumerate(zip(tops, weights, totals)):
            out = dot_nn(p.astype(bf16), y_ref[keys, head(2 * heads + h)]) / total
            send_ref[rows, head(heads + h)] = out.astype(bf16)
            tile = put_pieces(tile, lanes, CSTAT + 3 * h, m + jnp.log(total))
        tile = jnp.where(lanes < CSTAT, stat_ref[rows, :].astype(f32), tile)
        send_ref[rows, 2 * features :] = tile.astype(bf16)


def col_backward(y_ref, got_ref, sent_ref, bias_hbm, send_hbm, bias_t_ref, send_ref, sems):
    fetch = pltpu.make_async_copy(bias_hbm, bias_t_ref, sems.at[0])
    fetch.start()
    stores = []
    features = y_ref.shape[1] // 3
    heads = features // HEAD_DIM
    lanes = lanes_like(COLS)
    tile = jnp.where(
        lanes < CSTAT,
        got_ref[:, 2 * features :].astype(f32),
        sent_ref[:, 2 * features :].astype(f32),
    )
    for h in range(heads):
        product = got_ref[:, head(h)].astype(f32) * sent_ref[:, head(heads + h)].astype(f32)
        tile = jnp.where(lanes == 32 + h, jnp.sum(product, axis=1, keepdims=True), tile)
    tile = tile.T
    lses, dots = [], []
    for h in range(heads):
        row_lse = take_rows(tile, 6 * h)
        row_dots = take_rows(tile, 6 * h + 3)
        col_lse = take_rows(tile, CSTAT + 3 * h)
        col_dots = tile[32 + h : 33 + h]
        top = jnp.maximum(row_lse, col_lse)
        row_factor = jnp.exp(row_lse - top)
        col_factor = jnp.exp(col_lse - top)
        both = row_factor + col_factor
        lses.append(top + jnp.log(both))
        dots.append((row_dots * row_factor + col_dots * col_factor) / both)

    def store(rows, lanes):
        stores.append(
            pltpu.make_async_copy(
                send_ref.at[rows, lanes], send_hbm.at[rows, lanes], sems.at[len(stores) + 1]
            )
        )
        stores[-1].start()

    def part(ref, n):
        return lambda at, h: ref[at, head(n * heads + h)]

    gradients(
        part(y_ref, 0),
        part(y_ref, 1),
        part(y_ref, 2),
        part(got_ref, 0),
        lses,
        dots,
        lambda s, keys, rows: s + bias_t_ref[keys, rows].astype(f32),
        send_ref,
        heads,
        bf16,
        fetch.wait,
        store,
    )
    for copy in stores:
        copy.wait()


def gradients(q, k, v, g, lses, dots, masked, out_ref, heads, kind, ready=None, store=None):
    features = heads * HEAD_DIM
    grad_q = [None] * heads
    for start in range(COLS - BLOCK, -1, -BLOCK):
        keys = slice(start, start + BLOCK)
        rows = slice(start, COLS)
        products = [
            (dot_nt(k(keys, h), q(rows, h)) * SCALE, dot_nt(v(keys, h), g(rows, h))) for h in range(heads)
        ]
        if ready is not None:
            ready()
            ready = None
        for h, (s, d) in enumerate(products):
            p = jnp.exp(masked(s, keys, rows) - lses[h][:, start:])
            ds = (p * (d - dots[h][:, start:])).astype(bf16)
            out_ref[keys, head(2 * heads + h)] = dot_nn(p.astype(bf16), g(rows, h)).astype(kind)
            out_ref[keys, head(heads + h)] = (dot_nn(ds, q(rows, h)) * SCALE).astype(kind)
            term = dot_tn(ds, k(keys, h)) * SCALE
            if grad_q[h] is not None:
                term = term + jnp.concatenate([jnp.zeros((BLOCK, HEAD_DIM), f32), grad_q[h]], axis=0)
            grad_q[h] = term
        if store is not None:
            store(keys, slice(features, 3 * features))
    for h in range(heads):
        out_ref[:, head(h)] = grad_q[h].astype(kind)
    if store is not None:
        store(slice(0, COLS), slice(0, features))


def row_merge(core_ref, out_ref, sent_ref, got_ref, g_ref, weight_ref, att_ref, give_ref, merged_ref):
    features = g_ref.shape[1]
    heads = features // HEAD_DIM
    lanes = lanes_like(COLS)
    col_tile = got_ref[:, 2 * features :].astype(f32)
    merged = jnp.zeros((COLS, 128), f32)
    parts = []
    row_tile = sent_ref[:, 2 * features :].astype(f32)
    for h in range(heads):
        row_lse = take_lanes(row_tile, 6 * h)
        col_lse = take_lanes(col_tile, CSTAT + 3 * h)
        top = jnp.maximum(row_lse, col_lse)
        row_factor = jnp.exp(row_lse - top)
        col_factor = jnp.exp(col_lse - top)
        both = row_factor + col_factor
        att = (
            out_ref[:, head(h)] * row_factor + got_ref[:, head(heads + h)].astype(f32) * col_factor
        ) / both
        att = att.astype(bf16)
        parts.append(att)
        dots = jnp.sum(att.astype(f32) * g_ref[:, head(h)].astype(f32), axis=1, keepdims=True)
        merged = jnp.where(lanes == 2 * h, top + jnp.log(both), merged)
        merged = jnp.where(lanes == 2 * h + 1, dots, merged)
    merged_ref[...] = merged
    att_ref[...] = jnp.concatenate(parts, axis=1)
    project(1 - core_ref[0], att_ref, weight_ref, give_ref)


def project(core, att_ref, weight_ref, part_ref):
    features = att_ref.shape[1]
    for n in range(weight_ref.shape[1] // (2 * features)):
        at = pl.ds(pl.multiple_of((2 * n + core) * features, 128), features)
        part_ref[:, n * features : (n + 1) * features] = dot_nn(att_ref[...], weight_ref[:, at]).astype(bf16)


def project_own(core_ref, att_ref, weight_ref, part_ref):
    project(core_ref[0], att_ref, weight_ref, part_ref)


def pair_sum(x_ref, keep_ref, got_ref, own_ref, *send_refs):
    features = own_ref.shape[1]
    count = 1 + len(send_refs)
    for n, ref in enumerate((own_ref, *send_refs)):
        chip = lax.rem(x_ref[0] + n, count)
        at = pl.ds(pl.multiple_of(chip * features, 128), features)
        ref[...] = (keep_ref[:, at].astype(f32) + got_ref[:, at].astype(f32)).astype(ref.dtype)


def project_sum(own_ref, *refs):
    *part_refs, out_ref = refs
    total = own_ref[...]
    for ref in part_refs:
        total = total + ref[...].astype(f32)
    out_ref[...] = total.astype(bf16)


def row_backward(q_ref, k_ref, v_ref, g_ref, merged_ref, grad_ref):
    heads = q_ref.shape[1] // HEAD_DIM
    tile = merged_ref[...].T

    def masked(s, keys, rows):
        allowed = (lax.broadcasted_iota(jnp.int32, s.shape, 0) + keys.start) <= (
            lax.broadcasted_iota(jnp.int32, s.shape, 1) + rows.start
        )
        return jnp.where(allowed, s, NEG)

    def part(ref):
        return lambda at, h: ref[at, head(h)]

    gradients(
        part(q_ref),
        part(k_ref),
        part(v_ref),
        part(g_ref),
        [tile[2 * h : 2 * h + 1] for h in range(heads)],
        [tile[2 * h + 1 : 2 * h + 2] for h in range(heads)],
        masked,
        grad_ref,
        heads,
        f32,
    )


def finish(grad_ref, back_ref, q_ref, k_ref, v_ref):
    features = q_ref.shape[1]
    for n, ref in enumerate((q_ref, k_ref, v_ref)):
        at = slice(n * features, (n + 1) * features)
        ref[...] = (grad_ref[:, at] + back_ref[:, at].astype(f32)).astype(bf16)


def call(kernel, outs, cost, *args, far=(), far_out=(), scratch=(), room=16):
    vmem = pl.BlockSpec(memory_space=pltpu.VMEM)
    smem = pl.BlockSpec(memory_space=pltpu.SMEM)
    hbm = pl.BlockSpec(memory_space=pltpu.HBM)
    flops, exps = cost
    moved = sum(a.size * a.dtype.itemsize for a in args)
    moved += sum(o.size * o.dtype.itemsize for o in outs)
    return pl.pallas_call(
        kernel,
        out_shape=outs,
        in_specs=[smem if a.ndim == 1 else hbm if n in far else vmem for n, a in enumerate(args)],
        out_specs=[hbm if n in far_out else vmem for n in range(len(outs))],
        scratch_shapes=scratch,
        cost_estimate=pl.CostEstimate(flops=flops, bytes_accessed=moved, transcendentals=exps),
        compiler_params=pltpu.CompilerParams(vmem_limit_bytes=room * 1024 * 1024),
        name=getattr(kernel, "__name__", "pack"),
    )(*args)


def exchange(x):
    return lax.all_to_all(x, "seq", split_axis=0, concat_axis=0, tiled=True)


def local(queries, key_vectors, value_vectors, out_weight, attn_grad, tile_column_mask):
    tokens, features = queries.shape
    heads = features // HEAD_DIM
    width = COLS // lax.axis_size("seq")
    block = (lax.axis_index("seq") * width) // TILE
    mask = lax.dynamic_index_in_dim(tile_column_mask, block, 0, keepdims=False)
    product = 2 * COLS * COLS * HEAD_DIM * heads
    exps = COLS * COLS * heads

    def arr(columns, kind):
        return jax.ShapeDtypeStruct((tokens, columns), kind)

    def forward(queries, key_vectors, value_vectors, attn_grad, mask):
        return call(
            row_forward,
            [arr(features, f32), arr(128, bf16), arr(COLS, bf16), arr(COLS, bf16)],
            (2 * product, exps),
            queries, key_vectors, value_vectors, attn_grad, mask,
        )


    def packed(*pieces):
        def kernel(*refs):
            pack([p[1:] for p in pieces], refs)

        return call(
            kernel,
            [arr(sum(p[2] for p in pieces), bf16)],
            (0, 0),
            *[p[0] for p in pieces],
            far=range(len(pieces)),
            scratch=[pltpu.SemaphoreType.DMA((len(pieces),))],
        )[0]

    def at_once(queries, key_vectors, value_vectors, attn_grad, mask):
        qkv = exchange(
            packed((queries, 0, features), (key_vectors, 0, features), (value_vectors, 0, features))
        )
        row_out, row_stat, bias, bias_t = forward(queries, key_vectors, value_vectors, attn_grad, mask)
        (sent,) = call(
            col_forward,
            [arr(2 * features + 128, bf16)],
            (2 * product, exps),
            qkv, bias, attn_grad, row_stat,
        )
        return qkv, sent, row_out, bias_t

    def in_two(queries, key_vectors, value_vectors, attn_grad, mask):
        first = exchange(key_vectors[:, :HEAD_DIM])
        row_out, row_stat, bias, bias_t = forward(queries, key_vectors, value_vectors, attn_grad, mask)
        rest = packed(
            (queries, 0, features),
            (key_vectors, HEAD_DIM, features - HEAD_DIM),
            (value_vectors, 0, features),
        )
        rest, first = lax.optimization_barrier((rest, first))
        rest = exchange(rest)
        sent, qkv = call(
            col_forward_joined,
            [arr(2 * features + 128, bf16), arr(3 * features, bf16)],
            (2 * product, exps),
            first, rest, bias, attn_grad, row_stat,
        )
        return qkv, sent, row_out, bias_t

    place = lax.axis_index("tp")
    core = lax.rem(place, 2)
    qkv, sent, row_out, bias_t = lax.cond(
        core == 1, in_two, at_once, queries, key_vectors, value_vectors, attn_grad, mask
    )
    got = exchange(sent)
    (col_grads,) = call(
        col_backward, [arr(3 * features, bf16)], (5 * product, exps), qkv, got, sent, bias_t,
        far=(3,), far_out=(0,),
        scratch=[
            pltpu.VMEM((COLS, COLS), bf16),
            pltpu.VMEM((tokens, 3 * features), bf16),
            pltpu.SemaphoreType.DMA((2 + COLS // BLOCK,)),
        ],
    )
    back = exchange(col_grads)
    got, col_grads = lax.optimization_barrier((got, col_grads))
    half = out_weight.shape[1] // 2
    att, give, merged = call(
        row_merge,
        [arr(features, bf16), arr(half, bf16), arr(128, f32)],
        (2 * tokens * features * half, tokens),
        core.reshape(1), row_out, sent, got, attn_grad, out_weight,
    )
    count = lax.axis_size("tp")
    chips = count // 2
    pair = lax.ppermute(give, "tp", [(t, t ^ 1) for t in range(count)])
    (keep,) = call(
        project_own, [arr(half, bf16)], (2 * tokens * features * half, 0), core.reshape(1), att, out_weight
    )
    own, *sends = call(
        pair_sum,
        [arr(features, f32)] + [arr(features, bf16)] * (chips - 1),
        (tokens * half, 0),
        (place // 2).reshape(1), keep, pair,
    )
    far_first = sorted(range(1, chips), key=lambda n: -min(n, chips - n))
    parts = [
        lax.ppermute(sends[n - 1], "tp", [(t, (t + 2 * n) % count) for t in range(count)])
        for n in far_first
    ]
    (row_grads,) = call(
        row_backward, [arr(3 * features, f32)], (5 * product, exps),
        queries, key_vectors, value_vectors, attn_grad, merged,
    )
    (projected,) = call(project_sum, [arr(features, bf16)], (4 * tokens * features, 0), own, *parts)
    grads = call(finish, [arr(features, bf16)] * 3, (3 * tokens * features, 0), row_grads, back)
    return (projected, *grads)


def solution(mesh):
    return jax.shard_map(
        local,
        mesh=mesh,
        in_specs=(
            P("seq", "tp"),
            P("seq", "tp"),
            P("seq", "tp"),
            P("tp", None),
            P("seq", "tp"),
            P(),
        ),
        out_specs=(P("seq", "tp"), P("seq", "tp"), P("seq", "tp"), P("seq", "tp")),
        check_vma=False,
    )
```

```python
import jax
import jax.numpy as jnp
from jax import lax
from jax.experimental import pallas as pl
from jax.experimental.pallas import tpu as pltpu
from jax.sharding import PartitionSpec as P

HEAD_DIM = 128
COLS = 512
TILE = 128
SCALE = HEAD_DIM ** (-0.5)
NEG = -1e30
FORWARD_BLOCK = 512
BLOCK = 256
CSTAT = 64

bf16 = jnp.bfloat16
f32 = jnp.float32


def dot_nt(a, b):
    return lax.dot_general(a, b, (((1,), (1,)), ((), ())), preferred_element_type=f32)


def dot_tn(a, b):
    return lax.dot_general(a, b, (((0,), (0,)), ((), ())), preferred_element_type=f32)


def dot_nn(a, b):
    return jnp.dot(a, b, preferred_element_type=f32)


def head(h):
    return slice(h * HEAD_DIM, (h + 1) * HEAD_DIM)


def lanes_like(rows):
    return lax.broadcasted_iota(jnp.int32, (rows, 128), 1)


def put_pieces(tile, lanes, first, x):
    hi = x.astype(bf16).astype(f32)
    rest = x - hi
    mid = rest.astype(bf16).astype(f32)
    low = rest - mid
    for n, piece in enumerate((hi, mid, low)):
        tile = jnp.where(lanes == first + n, piece, tile)
    return tile


def take_lanes(tile, first):
    return tile[:, first : first + 1] + (tile[:, first + 1 : first + 2] + tile[:, first + 2 : first + 3])


def take_rows(tile, first):
    return tile[first : first + 1] + (tile[first + 1 : first + 2] + tile[first + 2 : first + 3])


def row_forward(q_ref, k_ref, v_ref, g_ref, mask_ref, out_ref, stat_ref, bias_ref, bias_t_ref):
    heads = q_ref.shape[1] // HEAD_DIM
    for start in range(0, COLS, FORWARD_BLOCK):
        rows = slice(start, start + FORWARD_BLOCK)
        keys = slice(0, start + FORWARD_BLOCK)
        allowed = lax.broadcasted_iota(jnp.int32, (FORWARD_BLOCK, start + FORWARD_BLOCK), 1) <= (
            lax.broadcasted_iota(jnp.int32, (FORWARD_BLOCK, start + FORWARD_BLOCK), 0) + start
        )
        lanes = lanes_like(FORWARD_BLOCK)
        tile = jnp.zeros((FORWARD_BLOCK, 128), f32)
        for h in range(heads):
            s = dot_nt(q_ref[rows, head(h)], k_ref[keys, head(h)]) * SCALE
            s = jnp.where(allowed, s, NEG)
            m = jnp.max(s, axis=1, keepdims=True)
            p = jnp.exp(s - m)
            total = jnp.sum(p, axis=1, keepdims=True)
            out = dot_nn(p.astype(bf16), v_ref[keys, head(h)]) / total
            out_ref[rows, head(h)] = out
            dots = jnp.sum(out * g_ref[rows, head(h)].astype(f32), axis=1, keepdims=True)
            tile = put_pieces(tile, lanes, 6 * h, m + jnp.log(total))
            tile = put_pieces(tile, lanes, 6 * h + 3, dots)
        stat_ref[rows, :] = tile.astype(bf16)
    pattern(mask_ref, bias_ref)
    pattern(mask_ref, bias_t_ref, turned=True)


def pattern(mask_ref, bias_ref, turned=False):
    total_rows = mask_ref.shape[0]
    width = COLS // total_rows
    mask = mask_ref[...].astype(f32).astype(bf16)
    spread = (
        lax.broadcasted_iota(jnp.int32, (COLS, total_rows), 0) // width
        == lax.broadcasted_iota(jnp.int32, (COLS, total_rows), 1)
    )
    spread = jnp.where(spread, 1.0, 0.0).astype(bf16)
    query = lax.broadcasted_iota(jnp.int32, (COLS, COLS), int(turned))
    key = lax.broadcasted_iota(jnp.int32, (COLS, COLS), 1 - int(turned))
    same = (query % width) == (key % width)
    rows = dot_nn(spread, mask).astype(bf16)
    whole = dot_nt(spread, rows) if turned else dot_nt(rows, spread)
    bias_ref[...] = jnp.where((whole > 0.5) & same & (key < query), 0.0, NEG).astype(bf16)


def pack(pieces, refs):
    *ins, out_ref, held_ref, sems = refs
    fetch, store = [], []
    at = 0
    for n, (ref, (first, width)) in enumerate(zip(ins, pieces)):
        held = held_ref.at[:, at : at + width]
        fetch.append(pltpu.make_async_copy(ref.at[:, first : first + width], held, sems.at[2 * n]))
        store.append(pltpu.make_async_copy(held, out_ref.at[:, at : at + width], sems.at[2 * n + 1]))
        at += width
    for copy in fetch:
        copy.start()
    for ready, copy in zip(fetch, store):
        ready.wait()
        copy.start()
    for copy in store:
        copy.wait()


def pack_first(core_ref, q_ref, k_ref, v_ref, first_ref, all_ref, held_ref, sems):
    features = q_ref.shape[1]

    @pl.when(core_ref[0] == 0)
    def _():
        pack([(0, features)] * 3, (q_ref, k_ref, v_ref, all_ref, held_ref, sems))

    @pl.when(core_ref[0] != 0)
    def _():
        pack([(0, HEAD_DIM)], (k_ref, first_ref, held_ref, sems))


def col_forward_joined(first_ref, rest_ref, bias_ref, g_ref, stat_ref, send_ref, y_ref):
    features = g_ref.shape[1]
    y_ref[:, :features] = rest_ref[:, :features]
    y_ref[:, features : features + HEAD_DIM] = first_ref[...]
    y_ref[:, features + HEAD_DIM :] = rest_ref[:, features:]
    col_forward(y_ref, bias_ref, g_ref, stat_ref, send_ref)


def col_forward(y_ref, bias_ref, g_ref, stat_ref, send_ref):
    features = g_ref.shape[1]
    heads = features // HEAD_DIM
    send_ref[:, :features] = g_ref[...]
    for start in range(0, COLS, FORWARD_BLOCK):
        rows = slice(start, start + FORWARD_BLOCK)
        keys = slice(0, start + FORWARD_BLOCK)
        lanes = lanes_like(FORWARD_BLOCK)
        tile = jnp.zeros((FORWARD_BLOCK, 128), f32)
        scores = [
            dot_nt(y_ref[rows, head(h)], y_ref[keys, head(heads + h)]) * SCALE
            + bias_ref[rows, keys].astype(f32)
            for h in range(heads)
        ]
        tops = [jnp.max(x, axis=1, keepdims=True) for x in scores]
        weights = [jnp.exp(x - m) for x, m in zip(scores, tops)]
        totals = [jnp.sum(p, axis=1, keepdims=True) for p in weights]
        for h, (m, p, total) in enumerate(zip(tops, weights, totals)):
            out = dot_nn(p.astype(bf16), y_ref[keys, head(2 * heads + h)]) / total
            send_ref[rows, head(heads + h)] = out.astype(bf16)
            tile = put_pieces(tile, lanes, CSTAT + 3 * h, m + jnp.log(total))
        tile = jnp.where(lanes < CSTAT, stat_ref[rows, :].astype(f32), tile)
        send_ref[rows, 2 * features :] = tile.astype(bf16)


def col_backward(y_ref, got_ref, sent_ref, bias_hbm, send_hbm, bias_t_ref, send_ref, sems):
    fetch = pltpu.make_async_copy(bias_hbm, bias_t_ref, sems.at[0])
    fetch.start()
    stores = []
    features = y_ref.shape[1] // 3
    heads = features // HEAD_DIM
    lanes = lanes_like(COLS)
    tile = jnp.where(
        lanes < CSTAT,
        got_ref[:, 2 * features :].astype(f32),
        sent_ref[:, 2 * features :].astype(f32),
    )
    for h in range(heads):
        product = got_ref[:, head(h)].astype(f32) * sent_ref[:, head(heads + h)].astype(f32)
        tile = jnp.where(lanes == 32 + h, jnp.sum(product, axis=1, keepdims=True), tile)
    tile = tile.T
    lses, dots = [], []
    for h in range(heads):
        row_lse = take_rows(tile, 6 * h)
        row_dots = take_rows(tile, 6 * h + 3)
        col_lse = take_rows(tile, CSTAT + 3 * h)
        col_dots = tile[32 + h : 33 + h]
        top = jnp.maximum(row_lse, col_lse)
        row_factor = jnp.exp(row_lse - top)
        col_factor = jnp.exp(col_lse - top)
        both = row_factor + col_factor
        lses.append(top + jnp.log(both))
        dots.append((row_dots * row_factor + col_dots * col_factor) / both)

    def store(rows, lanes):
        stores.append(
            pltpu.make_async_copy(
                send_ref.at[rows, lanes], send_hbm.at[rows, lanes], sems.at[len(stores) + 1]
            )
        )
        stores[-1].start()

    def part(ref, n):
        return lambda at, h: ref[at, head(n * heads + h)]

    gradients(
        part(y_ref, 0),
        part(y_ref, 1),
        part(y_ref, 2),
        part(got_ref, 0),
        lses,
        dots,
        lambda s, keys, rows: s + bias_t_ref[keys, rows].astype(f32),
        send_ref,
        heads,
        bf16,
        fetch.wait,
        store,
    )
    for copy in stores:
        copy.wait()


def gradients(q, k, v, g, lses, dots, masked, out_ref, heads, kind, ready=None, store=None):
    features = heads * HEAD_DIM
    grad_q = [None] * heads
    for start in range(COLS - BLOCK, -1, -BLOCK):
        keys = slice(start, start + BLOCK)
        rows = slice(start, COLS)
        products = [
            (dot_nt(k(keys, h), q(rows, h)) * SCALE, dot_nt(v(keys, h), g(rows, h))) for h in range(heads)
        ]
        if ready is not None:
            ready()
            ready = None
        for h, (s, d) in enumerate(products):
            p = jnp.exp(masked(s, keys, rows) - lses[h][:, start:])
            ds = (p * (d - dots[h][:, start:])).astype(bf16)
            out_ref[keys, head(2 * heads + h)] = dot_nn(p.astype(bf16), g(rows, h)).astype(kind)
            out_ref[keys, head(heads + h)] = (dot_nn(ds, q(rows, h)) * SCALE).astype(kind)
            term = dot_tn(ds, k(keys, h)) * SCALE
            if grad_q[h] is not None:
                term = term + jnp.concatenate([jnp.zeros((BLOCK, HEAD_DIM), f32), grad_q[h]], axis=0)
            grad_q[h] = term
        if store is not None:
            store(keys, slice(features, 3 * features))
    for h in range(heads):
        out_ref[:, head(h)] = grad_q[h].astype(kind)
    if store is not None:
        store(slice(0, COLS), slice(0, features))


def row_merge(core_ref, out_ref, sent_ref, got_ref, g_ref, weight_ref, att_ref, give_ref, merged_ref):
    features = g_ref.shape[1]
    heads = features // HEAD_DIM
    lanes = lanes_like(COLS)
    col_tile = got_ref[:, 2 * features :].astype(f32)
    merged = jnp.zeros((COLS, 128), f32)
    parts = []
    row_tile = sent_ref[:, 2 * features :].astype(f32)
    for h in range(heads):
        row_lse = take_lanes(row_tile, 6 * h)
        col_lse = take_lanes(col_tile, CSTAT + 3 * h)
        top = jnp.maximum(row_lse, col_lse)
        row_factor = jnp.exp(row_lse - top)
        col_factor = jnp.exp(col_lse - top)
        both = row_factor + col_factor
        att = (
            out_ref[:, head(h)] * row_factor + got_ref[:, head(heads + h)].astype(f32) * col_factor
        ) / both
        att = att.astype(bf16)
        parts.append(att)
        dots = jnp.sum(att.astype(f32) * g_ref[:, head(h)].astype(f32), axis=1, keepdims=True)
        merged = jnp.where(lanes == 2 * h, top + jnp.log(both), merged)
        merged = jnp.where(lanes == 2 * h + 1, dots, merged)
    merged_ref[...] = merged
    att_ref[...] = jnp.concatenate(parts, axis=1)
    project(1 - core_ref[0], att_ref, weight_ref, give_ref)


def project(core, att_ref, weight_ref, part_ref):
    features = att_ref.shape[1]
    for n in range(weight_ref.shape[1] // (2 * features)):
        at = pl.ds(pl.multiple_of((2 * n + core) * features, 128), features)
        part_ref[:, n * features : (n + 1) * features] = dot_nn(att_ref[...], weight_ref[:, at]).astype(bf16)


def project_own(core_ref, att_ref, weight_ref, part_ref):
    project(core_ref[0], att_ref, weight_ref, part_ref)


def pair_sum(x_ref, keep_ref, got_ref, own_ref, *send_refs):
    features = own_ref.shape[1]
    count = 1 + len(send_refs)
    for n, ref in enumerate((own_ref, *send_refs)):
        chip = lax.rem(x_ref[0] + n, count)
        at = pl.ds(pl.multiple_of(chip * features, 128), features)
        ref[...] = (keep_ref[:, at].astype(f32) + got_ref[:, at].astype(f32)).astype(ref.dtype)


def project_sum(own_ref, *refs):
    *part_refs, out_ref = refs
    total = own_ref[...]
    for ref in part_refs:
        total = total + ref[...].astype(f32)
    out_ref[...] = total.astype(bf16)


def row_backward(q_ref, k_ref, v_ref, g_ref, merged_ref, grad_ref):
    heads = q_ref.shape[1] // HEAD_DIM
    tile = merged_ref[...].T

    def masked(s, keys, rows):
        allowed = (lax.broadcasted_iota(jnp.int32, s.shape, 0) + keys.start) <= (
            lax.broadcasted_iota(jnp.int32, s.shape, 1) + rows.start
        )
        return jnp.where(allowed, s, NEG)

    def part(ref):
        return lambda at, h: ref[at, head(h)]

    gradients(
        part(q_ref),
        part(k_ref),
        part(v_ref),
        part(g_ref),
        [tile[2 * h : 2 * h + 1] for h in range(heads)],
        [tile[2 * h + 1 : 2 * h + 2] for h in range(heads)],
        masked,
        grad_ref,
        heads,
        f32,
    )


def finish(grad_ref, back_ref, q_ref, k_ref, v_ref):
    features = q_ref.shape[1]
    for n, ref in enumerate((q_ref, k_ref, v_ref)):
        at = slice(n * features, (n + 1) * features)
        ref[...] = (grad_ref[:, at] + back_ref[:, at].astype(f32)).astype(bf16)


def call(kernel, outs, cost, *args, far=(), far_out=(), scratch=(), room=16):
    vmem = pl.BlockSpec(memory_space=pltpu.VMEM)
    smem = pl.BlockSpec(memory_space=pltpu.SMEM)
    hbm = pl.BlockSpec(memory_space=pltpu.HBM)
    flops, exps = cost
    moved = sum(a.size * a.dtype.itemsize for a in args)
    moved += sum(o.size * o.dtype.itemsize for o in outs)
    return pl.pallas_call(
        kernel,
        out_shape=outs,
        in_specs=[smem if a.ndim == 1 else hbm if n in far else vmem for n, a in enumerate(args)],
        out_specs=[hbm if n in far_out else vmem for n in range(len(outs))],
        scratch_shapes=scratch,
        cost_estimate=pl.CostEstimate(flops=flops, bytes_accessed=moved, transcendentals=exps),
        compiler_params=pltpu.CompilerParams(vmem_limit_bytes=room * 1024 * 1024),
        name=getattr(kernel, "__name__", "pack"),
    )(*args)


def exchange(x):
    return lax.all_to_all(x, "seq", split_axis=0, concat_axis=0, tiled=True)


def local(queries, key_vectors, value_vectors, out_weight, attn_grad, tile_column_mask):
    tokens, features = queries.shape
    heads = features // HEAD_DIM
    width = COLS // lax.axis_size("seq")
    product = 2 * COLS * COLS * HEAD_DIM * heads
    exps = COLS * COLS * heads

    def arr(columns, kind):
        return jax.ShapeDtypeStruct((tokens, columns), kind)

    def forward(queries, key_vectors, value_vectors, attn_grad, mask):
        return call(
            row_forward,
            [arr(features, f32), arr(128, bf16), arr(COLS, bf16), arr(COLS, bf16)],
            (2 * product, exps),
            queries, key_vectors, value_vectors, attn_grad, mask,
        )


    def packed(*pieces):
        def kernel(*refs):
            pack([p[1:] for p in pieces], refs)

        return call(
            kernel,
            [arr(sum(p[2] for p in pieces), bf16)],
            (0, 0),
            *[p[0] for p in pieces],
            far=range(len(pieces)),
            far_out=(0,),
            scratch=[
                pltpu.VMEM((tokens, sum(p[2] for p in pieces)), bf16),
                pltpu.SemaphoreType.DMA((2 * len(pieces),)),
            ],
        )[0]

    def at_once(queries, key_vectors, value_vectors, attn_grad, mask, first, every):
        qkv = exchange(every)
        row_out, row_stat, bias, bias_t = forward(queries, key_vectors, value_vectors, attn_grad, mask)
        (sent,) = call(
            col_forward,
            [arr(2 * features + 128, bf16)],
            (2 * product, exps),
            qkv, bias, attn_grad, row_stat,
        )
        return qkv, sent, row_out, bias_t

    def in_two(queries, key_vectors, value_vectors, attn_grad, mask, first, every):
        first = exchange(first)
        row_out, row_stat, bias, bias_t = forward(queries, key_vectors, value_vectors, attn_grad, mask)
        rest = packed(
            (queries, 0, features),
            (key_vectors, HEAD_DIM, features - HEAD_DIM),
            (value_vectors, 0, features),
        )
        rest, first = lax.optimization_barrier((rest, first))
        rest = exchange(rest)
        sent, qkv = call(
            col_forward_joined,
            [arr(2 * features + 128, bf16), arr(3 * features, bf16)],
            (2 * product, exps),
            first, rest, bias, attn_grad, row_stat,
        )
        return qkv, sent, row_out, bias_t

    place = lax.axis_index("tp")
    core = lax.rem(place, 2)
    first, every = call(
        pack_first,
        [arr(HEAD_DIM, bf16), arr(3 * features, bf16)],
        (0, 0),
        core.reshape(1), queries, key_vectors, value_vectors,
        far=(1, 2, 3), far_out=(0, 1),
        scratch=[pltpu.VMEM((tokens, 3 * features), bf16), pltpu.SemaphoreType.DMA((6,))],
    )
    block, first = lax.optimization_barrier(((lax.axis_index("seq") * width) // TILE, first))
    mask = lax.dynamic_index_in_dim(tile_column_mask, block, 0, keepdims=False)
    qkv, sent, row_out, bias_t = lax.cond(
        core == 1, in_two, at_once, queries, key_vectors, value_vectors, attn_grad, mask, first, every
    )
    got = exchange(sent)
    (col_grads,) = call(
        col_backward, [arr(3 * features, bf16)], (5 * product, exps), qkv, got, sent, bias_t,
        far=(3,), far_out=(0,),
        scratch=[
            pltpu.VMEM((COLS, COLS), bf16),
            pltpu.VMEM((tokens, 3 * features), bf16),
            pltpu.SemaphoreType.DMA((2 + COLS // BLOCK,)),
        ],
    )
    back = exchange(col_grads)
    got, col_grads = lax.optimization_barrier((got, col_grads))
    half = out_weight.shape[1] // 2
    att, give, merged = call(
        row_merge,
        [arr(features, bf16), arr(half, bf16), arr(128, f32)],
        (2 * tokens * features * half, tokens),
        core.reshape(1), row_out, sent, got, attn_grad, out_weight,
    )
    count = lax.axis_size("tp")
    chips = count // 2
    pair = lax.ppermute(give, "tp", [(t, t ^ 1) for t in range(count)])
    (keep,) = call(
        project_own, [arr(half, bf16)], (2 * tokens * features * half, 0), core.reshape(1), att, out_weight
    )
    own, *sends = call(
        pair_sum,
        [arr(features, f32)] + [arr(features, bf16)] * (chips - 1),
        (tokens * half, 0),
        (place // 2).reshape(1), keep, pair,
    )
    far_first = sorted(range(1, chips), key=lambda n: -min(n, chips - n))
    parts = [
        lax.ppermute(sends[n - 1], "tp", [(t, (t + 2 * n) % count) for t in range(count)])
        for n in far_first
    ]
    (row_grads,) = call(
        row_backward, [arr(3 * features, f32)], (5 * product, exps),
        queries, key_vectors, value_vectors, attn_grad, merged,
    )
    (projected,) = call(project_sum, [arr(features, bf16)], (4 * tokens * features, 0), own, *parts)
    grads = call(finish, [arr(features, bf16)] * 3, (3 * tokens * features, 0), row_grads, back)
    return (projected, *grads)


def solution(mesh):
    return jax.shard_map(
        local,
        mesh=mesh,
        in_specs=(
            P("seq", "tp"),
            P("seq", "tp"),
            P("seq", "tp"),
            P("tp", None),
            P("seq", "tp"),
            P(),
        ),
        out_specs=(P("seq", "tp"), P("seq", "tp"), P("seq", "tp"), P("seq", "tp")),
        check_vma=False,
    )
```

```python
import jax
import jax.numpy as jnp
from jax import lax
from jax.experimental import pallas as pl
from jax.experimental.pallas import tpu as pltpu
from jax.sharding import PartitionSpec as P

HEAD_DIM = 128
COLS = 512
TILE = 128
SCALE = HEAD_DIM ** (-0.5)
NEG = -1e30
FORWARD_BLOCK = 512
BLOCK = 256
CSTAT = 64

bf16 = jnp.bfloat16
f32 = jnp.float32


def dot_nt(a, b):
    return lax.dot_general(a, b, (((1,), (1,)), ((), ())), preferred_element_type=f32)


def dot_tn(a, b):
    return lax.dot_general(a, b, (((0,), (0,)), ((), ())), preferred_element_type=f32)


def dot_nn(a, b):
    return jnp.dot(a, b, preferred_element_type=f32)


def head(h):
    return slice(h * HEAD_DIM, (h + 1) * HEAD_DIM)


def lanes_like(rows):
    return lax.broadcasted_iota(jnp.int32, (rows, 128), 1)


def put_pieces(tile, lanes, first, x):
    hi = x.astype(bf16).astype(f32)
    rest = x - hi
    mid = rest.astype(bf16).astype(f32)
    low = rest - mid
    for n, piece in enumerate((hi, mid, low)):
        tile = jnp.where(lanes == first + n, piece, tile)
    return tile


def take_lanes(tile, first):
    return tile[:, first : first + 1] + (tile[:, first + 1 : first + 2] + tile[:, first + 2 : first + 3])


def take_rows(tile, first):
    return tile[first : first + 1] + (tile[first + 1 : first + 2] + tile[first + 2 : first + 3])


def row_forward(q_ref, k_ref, v_ref, g_ref, mask_ref, out_ref, stat_ref, bias_ref, bias_t_ref):
    heads = q_ref.shape[1] // HEAD_DIM
    for start in range(0, COLS, FORWARD_BLOCK):
        rows = slice(start, start + FORWARD_BLOCK)
        keys = slice(0, start + FORWARD_BLOCK)
        allowed = lax.broadcasted_iota(jnp.int32, (FORWARD_BLOCK, start + FORWARD_BLOCK), 1) <= (
            lax.broadcasted_iota(jnp.int32, (FORWARD_BLOCK, start + FORWARD_BLOCK), 0) + start
        )
        lanes = lanes_like(FORWARD_BLOCK)
        tile = jnp.zeros((FORWARD_BLOCK, 128), f32)
        for h in range(heads):
            s = dot_nt(q_ref[rows, head(h)], k_ref[keys, head(h)]) * SCALE
            s = jnp.where(allowed, s, NEG)
            m = jnp.max(s, axis=1, keepdims=True)
            p = jnp.exp(s - m)
            total = jnp.sum(p, axis=1, keepdims=True)
            out = dot_nn(p.astype(bf16), v_ref[keys, head(h)]) / total
            out_ref[rows, head(h)] = out
            dots = jnp.sum(out * g_ref[rows, head(h)].astype(f32), axis=1, keepdims=True)
            tile = put_pieces(tile, lanes, 6 * h, m + jnp.log(total))
            tile = put_pieces(tile, lanes, 6 * h + 3, dots)
        stat_ref[rows, :] = tile.astype(bf16)
    pattern(mask_ref, bias_ref)
    pattern(mask_ref, bias_t_ref, turned=True)


def pattern(mask_ref, bias_ref, turned=False):
    total_rows = mask_ref.shape[0]
    width = COLS // total_rows
    mask = mask_ref[...].astype(f32).astype(bf16)
    spread = (
        lax.broadcasted_iota(jnp.int32, (COLS, total_rows), 0) // width
        == lax.broadcasted_iota(jnp.int32, (COLS, total_rows), 1)
    )
    spread = jnp.where(spread, 1.0, 0.0).astype(bf16)
    query = lax.broadcasted_iota(jnp.int32, (COLS, COLS), int(turned))
    key = lax.broadcasted_iota(jnp.int32, (COLS, COLS), 1 - int(turned))
    same = (query % width) == (key % width)
    rows = dot_nn(spread, mask).astype(bf16)
    whole = dot_nt(spread, rows) if turned else dot_nt(rows, spread)
    bias_ref[...] = jnp.where((whole > 0.5) & same & (key < query), 0.0, NEG).astype(bf16)


def pack(pieces, refs):
    *ins, out_ref, held_ref, sems = refs
    fetch, store = [], []
    at = 0
    for n, (ref, (first, width)) in enumerate(zip(ins, pieces)):
        held = held_ref.at[:, at : at + width]
        fetch.append(pltpu.make_async_copy(ref.at[:, first : first + width], held, sems.at[2 * n]))
        store.append(pltpu.make_async_copy(held, out_ref.at[:, at : at + width], sems.at[2 * n + 1]))
        at += width
    for copy in fetch:
        copy.start()
    for ready, copy in zip(fetch, store):
        ready.wait()
        copy.start()
    for copy in store:
        copy.wait()


def pack_first(core_ref, q_ref, k_ref, v_ref, first_ref, all_ref, held_ref, sems):
    features = q_ref.shape[1]

    @pl.when(core_ref[0] == 0)
    def _():
        pack([(0, features)] * 3, (q_ref, k_ref, v_ref, all_ref, held_ref, sems))

    @pl.when(core_ref[0] != 0)
    def _():
        pack([(0, HEAD_DIM)], (k_ref, first_ref, held_ref, sems))


def col_forward_joined(first_ref, rest_ref, bias_ref, g_ref, stat_ref, send_ref, y_ref):
    features = g_ref.shape[1]
    y_ref[:, :features] = rest_ref[:, :features]
    y_ref[:, features : features + HEAD_DIM] = first_ref[...]
    y_ref[:, features + HEAD_DIM :] = rest_ref[:, features:]
    col_forward(y_ref, bias_ref, g_ref, stat_ref, send_ref)


def col_forward(y_ref, bias_ref, g_ref, stat_ref, send_ref):
    features = g_ref.shape[1]
    heads = features // HEAD_DIM
    send_ref[:, :features] = g_ref[...]
    for start in range(0, COLS, FORWARD_BLOCK):
        rows = slice(start, start + FORWARD_BLOCK)
        keys = slice(0, start + FORWARD_BLOCK)
        lanes = lanes_like(FORWARD_BLOCK)
        tile = jnp.zeros((FORWARD_BLOCK, 128), f32)
        scores = [
            dot_nt(y_ref[rows, head(h)], y_ref[keys, head(heads + h)]) * SCALE
            + bias_ref[rows, keys].astype(f32)
            for h in range(heads)
        ]
        tops = [jnp.max(x, axis=1, keepdims=True) for x in scores]
        weights = [jnp.exp(x - m) for x, m in zip(scores, tops)]
        totals = [jnp.sum(p, axis=1, keepdims=True) for p in weights]
        for h, (m, p, total) in enumerate(zip(tops, weights, totals)):
            out = dot_nn(p.astype(bf16), y_ref[keys, head(2 * heads + h)]) / total
            send_ref[rows, head(heads + h)] = out.astype(bf16)
            tile = put_pieces(tile, lanes, CSTAT + 3 * h, m + jnp.log(total))
        tile = jnp.where(lanes < CSTAT, stat_ref[rows, :].astype(f32), tile)
        send_ref[rows, 2 * features :] = tile.astype(bf16)


def col_backward(y_ref, got_ref, sent_ref, bias_hbm, send_hbm, bias_t_ref, send_ref, sems):
    fetch = pltpu.make_async_copy(bias_hbm, bias_t_ref, sems.at[0])
    fetch.start()
    stores = []
    features = y_ref.shape[1] // 3
    heads = features // HEAD_DIM
    lanes = lanes_like(COLS)
    tile = jnp.where(
        lanes < CSTAT,
        got_ref[:, 2 * features :].astype(f32),
        sent_ref[:, 2 * features :].astype(f32),
    )
    for h in range(heads):
        product = got_ref[:, head(h)].astype(f32) * sent_ref[:, head(heads + h)].astype(f32)
        tile = jnp.where(lanes == 32 + h, jnp.sum(product, axis=1, keepdims=True), tile)
    tile = tile.T
    lses, dots = [], []
    for h in range(heads):
        row_lse = take_rows(tile, 6 * h)
        row_dots = take_rows(tile, 6 * h + 3)
        col_lse = take_rows(tile, CSTAT + 3 * h)
        col_dots = tile[32 + h : 33 + h]
        top = jnp.maximum(row_lse, col_lse)
        row_factor = jnp.exp(row_lse - top)
        col_factor = jnp.exp(col_lse - top)
        both = row_factor + col_factor
        lses.append(top + jnp.log(both))
        dots.append((row_dots * row_factor + col_dots * col_factor) / both)

    def store(rows, lanes):
        stores.append(
            pltpu.make_async_copy(
                send_ref.at[rows, lanes], send_hbm.at[rows, lanes], sems.at[len(stores) + 1]
            )
        )
        stores[-1].start()

    def part(ref, n):
        return lambda at, h: ref[at, head(n * heads + h)]

    gradients(
        part(y_ref, 0),
        part(y_ref, 1),
        part(y_ref, 2),
        part(got_ref, 0),
        lses,
        dots,
        lambda s, keys, rows: s + bias_t_ref[keys, rows].astype(f32),
        send_ref,
        heads,
        bf16,
        fetch.wait,
        store,
    )
    for copy in stores:
        copy.wait()


def gradients(q, k, v, g, lses, dots, masked, out_ref, heads, kind, ready=None, store=None):
    features = heads * HEAD_DIM
    grad_q = [None] * heads
    for start in range(COLS - BLOCK, -1, -BLOCK):
        keys = slice(start, start + BLOCK)
        rows = slice(start, COLS)
        products = [
            (dot_nt(k(keys, h), q(rows, h)) * SCALE, dot_nt(v(keys, h), g(rows, h))) for h in range(heads)
        ]
        if ready is not None:
            ready()
            ready = None
        for h, (s, d) in enumerate(products):
            p = jnp.exp(masked(s, keys, rows) - lses[h][:, start:])
            ds = (p * (d - dots[h][:, start:])).astype(bf16)
            out_ref[keys, head(2 * heads + h)] = dot_nn(p.astype(bf16), g(rows, h)).astype(kind)
            out_ref[keys, head(heads + h)] = (dot_nn(ds, q(rows, h)) * SCALE).astype(kind)
            term = dot_tn(ds, k(keys, h)) * SCALE
            if grad_q[h] is not None:
                term = term + jnp.concatenate([jnp.zeros((BLOCK, HEAD_DIM), f32), grad_q[h]], axis=0)
            grad_q[h] = term
        if store is not None:
            store(keys, slice(features, 3 * features))
    for h in range(heads):
        out_ref[:, head(h)] = grad_q[h].astype(kind)
    if store is not None:
        store(slice(0, COLS), slice(0, features))


def row_merge(core_ref, out_ref, sent_ref, got_ref, g_ref, weight_ref, att_ref, give_ref, merged_ref):
    features = g_ref.shape[1]
    heads = features // HEAD_DIM
    lanes = lanes_like(COLS)
    col_tile = got_ref[:, 2 * features :].astype(f32)
    merged = jnp.zeros((COLS, 128), f32)
    parts = []
    row_tile = sent_ref[:, 2 * features :].astype(f32)
    for h in range(heads):
        row_lse = take_lanes(row_tile, 6 * h)
        col_lse = take_lanes(col_tile, CSTAT + 3 * h)
        top = jnp.maximum(row_lse, col_lse)
        row_factor = jnp.exp(row_lse - top)
        col_factor = jnp.exp(col_lse - top)
        both = row_factor + col_factor
        att = (
            out_ref[:, head(h)] * row_factor + got_ref[:, head(heads + h)].astype(f32) * col_factor
        ) / both
        att = att.astype(bf16)
        parts.append(att)
        dots = jnp.sum(att.astype(f32) * g_ref[:, head(h)].astype(f32), axis=1, keepdims=True)
        merged = jnp.where(lanes == 2 * h, top + jnp.log(both), merged)
        merged = jnp.where(lanes == 2 * h + 1, dots, merged)
    merged_ref[...] = merged
    att_ref[...] = jnp.concatenate(parts, axis=1)
    project(1 - core_ref[0], att_ref, weight_ref, give_ref)


def project(core, att_ref, weight_ref, part_ref):
    features = att_ref.shape[1]
    for n in range(weight_ref.shape[1] // (2 * features)):
        at = pl.ds(pl.multiple_of((2 * n + core) * features, 128), features)
        part_ref[:, n * features : (n + 1) * features] = dot_nn(att_ref[...], weight_ref[:, at]).astype(bf16)


def project_own(core_ref, att_ref, weight_ref, part_ref):
    project(core_ref[0], att_ref, weight_ref, part_ref)


def pair_sum(x_ref, keep_ref, got_ref, own_ref, *send_refs):
    features = own_ref.shape[1]
    count = 1 + len(send_refs)
    for n, ref in enumerate((own_ref, *send_refs)):
        chip = lax.rem(x_ref[0] + n, count)
        at = pl.ds(pl.multiple_of(chip * features, 128), features)
        ref[...] = (keep_ref[:, at].astype(f32) + got_ref[:, at].astype(f32)).astype(ref.dtype)


def project_sum(own_ref, *refs):
    *part_refs, out_ref = refs
    total = own_ref[...]
    for ref in part_refs:
        total = total + ref[...].astype(f32)
    out_ref[...] = total.astype(bf16)


def row_backward(q_ref, k_ref, v_ref, g_ref, merged_ref, grad_ref):
    heads = q_ref.shape[1] // HEAD_DIM
    tile = merged_ref[...].T

    def masked(s, keys, rows):
        allowed = (lax.broadcasted_iota(jnp.int32, s.shape, 0) + keys.start) <= (
            lax.broadcasted_iota(jnp.int32, s.shape, 1) + rows.start
        )
        return jnp.where(allowed, s, NEG)

    def part(ref):
        return lambda at, h: ref[at, head(h)]

    gradients(
        part(q_ref),
        part(k_ref),
        part(v_ref),
        part(g_ref),
        [tile[2 * h : 2 * h + 1] for h in range(heads)],
        [tile[2 * h + 1 : 2 * h + 2] for h in range(heads)],
        masked,
        grad_ref,
        heads,
        f32,
    )


def finish(grad_ref, back_ref, q_ref, k_ref, v_ref):
    features = q_ref.shape[1]
    for n, ref in enumerate((q_ref, k_ref, v_ref)):
        at = slice(n * features, (n + 1) * features)
        ref[...] = (grad_ref[:, at] + back_ref[:, at].astype(f32)).astype(bf16)


def call(kernel, outs, cost, *args, far=(), far_out=(), scratch=(), room=16):
    vmem = pl.BlockSpec(memory_space=pltpu.VMEM)
    smem = pl.BlockSpec(memory_space=pltpu.SMEM)
    hbm = pl.BlockSpec(memory_space=pltpu.HBM)
    flops, exps = cost
    moved = sum(a.size * a.dtype.itemsize for a in args)
    moved += sum(o.size * o.dtype.itemsize for o in outs)
    return pl.pallas_call(
        kernel,
        out_shape=outs,
        in_specs=[smem if a.ndim == 1 else hbm if n in far else vmem for n, a in enumerate(args)],
        out_specs=[hbm if n in far_out else vmem for n in range(len(outs))],
        scratch_shapes=scratch,
        cost_estimate=pl.CostEstimate(flops=flops, bytes_accessed=moved, transcendentals=exps),
        compiler_params=pltpu.CompilerParams(vmem_limit_bytes=room * 1024 * 1024),
        name=getattr(kernel, "__name__", "pack"),
    )(*args)


def exchange(x):
    return lax.all_to_all(x, "seq", split_axis=0, concat_axis=0, tiled=True)


def local(queries, key_vectors, value_vectors, out_weight, attn_grad, tile_column_mask):
    tokens, features = queries.shape
    heads = features // HEAD_DIM
    width = COLS // lax.axis_size("seq")
    product = 2 * COLS * COLS * HEAD_DIM * heads
    exps = COLS * COLS * heads

    def arr(columns, kind):
        return jax.ShapeDtypeStruct((tokens, columns), kind)

    def forward(queries, key_vectors, value_vectors, attn_grad, mask):
        return call(
            row_forward,
            [arr(features, f32), arr(128, bf16), arr(COLS, bf16), arr(COLS, bf16)],
            (2 * product, exps),
            queries, key_vectors, value_vectors, attn_grad, mask,
        )


    def packed(*pieces):
        def kernel(*refs):
            pack([p[1:] for p in pieces], refs)

        return call(
            kernel,
            [arr(sum(p[2] for p in pieces), bf16)],
            (0, 0),
            *[p[0] for p in pieces],
            far=range(len(pieces)),
            far_out=(0,),
            scratch=[
                pltpu.VMEM((tokens, sum(p[2] for p in pieces)), bf16),
                pltpu.SemaphoreType.DMA((2 * len(pieces),)),
            ],
        )[0]

    def at_once(queries, key_vectors, value_vectors, attn_grad, mask, first, every):
        qkv = exchange(every)
        row_out, row_stat, bias, bias_t = forward(queries, key_vectors, value_vectors, attn_grad, mask)
        (sent,) = call(
            col_forward,
            [arr(2 * features + 128, bf16)],
            (2 * product, exps),
            qkv, bias, attn_grad, row_stat,
        )
        return qkv, sent, row_out, bias_t

    def in_two(queries, key_vectors, value_vectors, attn_grad, mask, first, every):
        first = exchange(first)
        row_out, row_stat, bias, bias_t = forward(queries, key_vectors, value_vectors, attn_grad, mask)
        rest = packed(
            (queries, 0, features),
            (key_vectors, HEAD_DIM, features - HEAD_DIM),
            (value_vectors, 0, features),
        )
        rest, first = lax.optimization_barrier((rest, first))
        rest = exchange(rest)
        sent, qkv = call(
            col_forward_joined,
            [arr(2 * features + 128, bf16), arr(3 * features, bf16)],
            (2 * product, exps),
            first, rest, bias, attn_grad, row_stat,
        )
        return qkv, sent, row_out, bias_t

    place = lax.axis_index("tp")
    core = lax.rem(place, 2)
    first, every = call(
        pack_first,
        [arr(HEAD_DIM, bf16), arr(3 * features, bf16)],
        (0, 0),
        core.reshape(1), queries, key_vectors, value_vectors,
        far=(1, 2, 3), far_out=(0, 1),
        scratch=[pltpu.VMEM((tokens, 3 * features), bf16), pltpu.SemaphoreType.DMA((6,))],
    )
    block, first = lax.optimization_barrier(((lax.axis_index("seq") * width) // TILE, first))
    mask = lax.dynamic_index_in_dim(tile_column_mask, block, 0, keepdims=False)
    qkv, sent, row_out, bias_t = lax.cond(
        core == 1, in_two, at_once, queries, key_vectors, value_vectors, attn_grad, mask, first, every
    )
    got = exchange(sent)
    (col_grads,) = call(
        col_backward, [arr(3 * features, bf16)], (5 * product, exps), qkv, got, sent, bias_t,
        far=(3,), far_out=(0,),
        scratch=[
            pltpu.VMEM((COLS, COLS), bf16),
            pltpu.VMEM((tokens, 3 * features), bf16),
            pltpu.SemaphoreType.DMA((2 + COLS // BLOCK,)),
        ],
    )
    back = exchange(col_grads)
    got, col_grads = lax.optimization_barrier((got, col_grads))
    half = out_weight.shape[1] // 2
    att, give, merged = call(
        row_merge,
        [arr(features, bf16), arr(half, bf16), arr(128, f32)],
        (2 * tokens * features * half, tokens),
        core.reshape(1), row_out, sent, got, attn_grad, out_weight,
    )
    count = lax.axis_size("tp")
    chips = count // 2
    pair = lax.ppermute(give, "tp", [(t, t ^ 1) for t in range(count)])
    (keep,) = call(
        project_own, [arr(half, bf16)], (2 * tokens * features * half, 0), core.reshape(1), att, out_weight
    )
    own, *sends = call(
        pair_sum,
        [arr(features, f32)] + [arr(features, bf16)] * (chips - 1),
        (tokens * half, 0),
        (place // 2).reshape(1), keep, pair,
    )
    near_first = sorted(range(1, chips), key=lambda n: min(n, chips - n))
    parts = [
        lax.ppermute(sends[n - 1], "tp", [(t, (t + 2 * n) % count) for t in range(count)])
        for n in near_first
    ]
    (row_grads,) = call(
        row_backward, [arr(3 * features, f32)], (5 * product, exps),
        queries, key_vectors, value_vectors, attn_grad, merged,
    )
    (projected,) = call(project_sum, [arr(features, bf16)], (4 * tokens * features, 0), own, *parts)
    grads = call(finish, [arr(features, bf16)] * 3, (3 * tokens * features, 0), row_grads, back)
    return (projected, *grads)


def solution(mesh):
    return jax.shard_map(
        local,
        mesh=mesh,
        in_specs=(
            P("seq", "tp"),
            P("seq", "tp"),
            P("seq", "tp"),
            P("tp", None),
            P("seq", "tp"),
            P(),
        ),
        out_specs=(P("seq", "tp"), P("seq", "tp"), P("seq", "tp"), P("seq", "tp")),
        check_vma=False,
    )
```
